32 devices in a mesh: tm: 4 (over y, x), area: 8 (over z, core).
Axes of the slice: x: 2, y: 2, z: 4, core: 2. Of those that a mesh axis runs over, the one named last changes fastest.
Arguments:
- gradient: float32 [168, 32, 512], P('tm', 'area'), may hold values from -72 to 72
- barrier: float32 [1], replicated, may hold values from 0.5 to 2
- slack: float32 [168, 32, 512], P('tm', 'area'), may hold values from 0.5 to 2
- hess_diag: float32 [168, 32, 512], P('tm', 'area'), may hold values from 0.5 to 2
- tile: float32 [32, 512, 512], P('area'), may hold values from -0.1 to 4.1, as said below
- ramp_weight: float32 [32, 512], P('area'), may hold values from 0.5 to 2
- bus_coupling: float32 [32, 512], P('area'), may hold values from 0.5 to 2
- tie_offset: int32 [32, 4], replicated, may hold values from 1 to 4, as said below
- tie_admittance: float32 [32, 4], replicated, may hold values from 0.5 to 2
- con_sens: float32 [2048, 512], P('area'), may hold values from -0.9 to 0.9
- con_weight: float32 [2048, 168], P('area', 'tm'), may hold values from 0.5 to 2
- con_owner: int32 [2048, 1], P('area'), may hold values from 0 to 31; in each aligned block of 256 rows (0 to 255, 256 to 511, ...) at most 16 rows name the same one
- step_guess: float32 [168, 32, 512], P('tm', 'area'), may hold values from -1.2 to 1.2
Outputs:
- newton_step: float32 [168, 32, 512], P('tm', 'area')
- residual: float32 [168, 32, 512], P('tm', 'area')
The draws below stay inside these ranges and needn't reach their ends.
Inputs may be any that keep to these rules, and one draw needn't show every extreme that they name: `tie_offset`: each tie partner lies 1 to 4 areas above its area; a partner past the last area is absent. `con_owner`: on the rows of one index of area, no area owns more than 16 blocks. Each area's tile is symmetric.
All inputs are finite; a program needn't handle non-finite values.
Results may differ from the reference program's by a relative error of at most 0.00028.
Values sent between devices are 32-bit elements; how exact they have to be, the bound alone decides.
No kernel may reach another device: no remote copies, remote signals or barrier semaphores. Data moves between devices by JAX's collectives and lax.ppermute only.
A program may use at most 64 MiB of HBM per device.

```python
import math
import jax
import jax.numpy as jnp
import numpy as np
from jax import lax

NV = 512
TIES = 4
ITERS = 2
AREA_DEV = 4
NCON_DEV = 256
HOURS = 168
AREAS = 32
NCON = 2048
CAP = 16


def draw_gradient(key, part):
    area_scale = 1.0 + 2.0 * jnp.arange(AREAS, dtype=jnp.float32) / max(AREAS - 1, 1)
    values = jnp.clip(jax.random.normal(key, (HOURS, AREAS, NV), jnp.float32), -6.0, 6.0)
    return 4.0 * values * area_scale[None, :, None]


def draw_tile(key, part):
    values = jax.random.uniform(key, (AREAS, NV, NV), jnp.float32, -0.1, 0.1)
    mirrored = 0.5 * (values + jnp.swapaxes(values, 1, 2))
    return mirrored + 4.0 * jnp.eye(NV, dtype=jnp.float32)[None]


def draw_tie_offset(key, part):
    values = jax.random.randint(key, (AREAS, TIES), 1, AREA_DEV + 1, dtype=jnp.int32)
    values = values.at[0, 0].set(AREA_DEV)
    return values.at[0, 1].set(1)


def level_of(own_key, shape, split, least, high):
    factor_of = 1.0
    for dim, parts in split:
        heights = jax.random.uniform(jax.random.fold_in(jax.random.fold_in(own_key, 6), dim), (parts,), jnp.float32, least / len(split), high / len(split))
        factor_of = factor_of * jnp.repeat(jnp.exp(heights), shape[dim] // parts).reshape((-1,) + (1,) * (len(shape) - 1 - dim))
    return factor_of


def deal_out(rng, own, number, rows, amount, top, reach, skew):
    ranking = jax.random.permutation(rng, amount)
    heavy_load, usual = load_shares(amount, rows * top, reach, skew, True), load_shares(amount, rows * top, reach, skew, False)
    places = jnp.arange(amount)

    def named(tallies, rotation):
        used = int((tallies > 0).sum())
        fixed = max(1, used // 4)
        shifted = fixed + (places - fixed + rotation * (used - fixed)) % max(1, amount - fixed)
        return jnp.zeros((amount,), jnp.int32).at[ranking[jnp.where(places < fixed, places, shifted)]].set(jnp.asarray(tallies, jnp.int32))

    tallies = jnp.where(number % 4 == 0, named(heavy_load, number // 4), named(usual, number - number // 4 - 1))
    mixed = jax.random.permutation(jax.random.fold_in(own, 3), amount)
    giver, taker = mixed[0:amount // 2 * 2:2], mixed[1:amount // 2 * 2:2]
    room = jnp.minimum(tallies[giver] - 1, reach - tallies[taker]) // 2
    room = jnp.where((giver == ranking[0]) | (taker == ranking[0]) | (tallies[taker] == 0), 0, jnp.maximum(room, 0))
    shifted = jax.random.randint(jax.random.fold_in(own, 4), (amount // 2,), 0, 1 << 20) % (room + 1)
    tallies = tallies.at[giver].add(-shifted).at[taker].add(shifted)
    members = jnp.searchsorted(jnp.cumsum(tallies), jnp.arange(rows * top), side="right").astype(jnp.int32)
    table = members.reshape(top, rows).T
    table = table[jax.random.permutation(jax.random.fold_in(own, 1), rows)]
    rotation = jax.random.randint(jax.random.fold_in(own, 2), (rows, 1), 0, top)
    return jnp.take_along_axis(table, (jnp.arange(top)[None, :] + rotation) % top, axis=1)


def load_shares(count, total, bound, lean, full):
    loads = [(1 << 20) // math.isqrt(standing ** lean) + 1 for standing in range(1, count + 1)]
    largest = bound if full else min(bound, max(-(-total // count), total * loads[0] // sum(loads)))
    least = 1 if total - largest >= count - 1 else 0
    holding, spare = [largest] + [least] * (count - 1), total - largest - least * (count - 1)
    while spare > 0:
        free = [i for i in range(1, count) if holding[i] < largest] or [i for i in range(1, count) if holding[i] < bound]
        pool, remaining = sum([loads[i] for i in free]), spare
        for i in free:
            extra = min(bound - holding[i], max(1, remaining * loads[i] // pool), spare)
            holding[i] = holding[i] + extra
            spare = spare - extra
    return np.array(holding)


def bell_draw(own_key, shape, spread, bound, cuts=(), kind=jnp.bfloat16):
    drawn = jax.random.normal(own_key, shape, jnp.float32) * spread
    if len(cuts) > 0:
        drawn = level_of(own_key, shape, cuts, -0.22, 0.18) * drawn
    return jnp.clip(drawn, min=-bound, max=bound).astype(kind)


def setup_inputs(seed: int = 0) -> dict:
    streams_of = jax.random.split(jax.random.key(seed), 14)
    gradient = draw_gradient(jax.random.fold_in(streams_of[13], 71), 0)
    barrier = jnp.clip(jnp.exp(jax.random.uniform(streams_of[1], (1,), jnp.float32, math.log(0.5), math.log(2.0))), 0.5, 2.0)
    slack = jnp.clip(jnp.exp(math.log(2.0) - 1.3862944 * jax.random.uniform(streams_of[2], (HOURS, AREAS, NV), jnp.float32) ** level_of(streams_of[2], (HOURS, AREAS, NV), ((0, 4), (1, 8)), -0.2, 0.2)), 0.5, 2.0)
    hess_diag = jnp.clip(jnp.exp(math.log(2.0) - 1.3862944 * jax.random.uniform(streams_of[3], (HOURS, AREAS, NV), jnp.float32) ** level_of(streams_of[3], (HOURS, AREAS, NV), ((0, 4), (1, 8)), -0.2, 0.2)), 0.5, 2.0)
    tile = draw_tile(jax.random.fold_in(streams_of[13], 71), 0)
    ramp_weight = jnp.clip(jnp.exp(math.log(2.0) - 1.3862944 * jax.random.uniform(streams_of[5], (AREAS, NV), jnp.float32) ** level_of(streams_of[5], (AREAS, NV), ((0, 8),), -0.2, 0.2)), 0.5, 2.0)
    bus_coupling = jnp.clip(jnp.exp(math.log(2.0) - 1.3862944 * jax.random.uniform(streams_of[6], (AREAS, NV), jnp.float32) ** level_of(streams_of[6], (AREAS, NV), ((0, 8),), -0.2, 0.2)), 0.5, 2.0)
    tie_offset = draw_tie_offset(jax.random.fold_in(streams_of[13], 71), 0)
    tie_admittance = jnp.clip(jnp.exp(jax.random.uniform(streams_of[8], (AREAS, TIES), jnp.float32, math.log(0.5), math.log(2.0))), 0.5, 2.0)
    con_sens = bell_draw(streams_of[9], (NCON, NV), 0.15, 0.9, ((0, 8),), jnp.float32)
    con_weight = jnp.clip(jnp.exp(math.log(2.0) - 1.3862944 * jax.random.uniform(streams_of[10], (NCON, HOURS), jnp.float32) ** level_of(streams_of[10], (NCON, HOURS), ((0, 8), (1, 4)), -0.2, 0.2)), 0.5, 2.0)
    con_owner_keys = jax.random.split(jax.random.fold_in(streams_of[11], 1), NCON // NCON_DEV)
    con_owner_turns = jax.random.permutation(jax.random.fold_in(streams_of[11], 3), NCON // NCON_DEV)
    con_owner = jax.vmap(lambda own, number: deal_out(jax.random.fold_in(streams_of[11], 2), own, number, NCON_DEV, AREAS, 1, CAP, 2))(con_owner_keys, con_owner_turns).reshape((NCON, 1))
    step_guess = bell_draw(streams_of[12], (HOURS, AREAS, NV), 0.2, 1.2, ((0, 4), (1, 8)), jnp.float32)
    return dict(gradient=gradient, barrier=barrier, slack=slack, hess_diag=hess_diag, tile=tile, ramp_weight=ramp_weight, bus_coupling=bus_coupling, tie_offset=tie_offset, tie_admittance=tie_admittance, con_sens=con_sens, con_weight=con_weight, con_owner=con_owner, step_guess=step_guess)


def tie_product(input_vector, bus_coupling, tie_offset, tie_admittance):
    area_count = input_vector.shape[1]
    summed = jnp.zeros_like(input_vector)
    positions = jnp.arange(area_count, dtype=jnp.int32)
    for column in range(TIES):
        target = positions + tie_offset[:, column].astype(jnp.int32)
        inside = target < area_count
        clipped = jnp.minimum(target, area_count - 1).astype(jnp.int32)
        far_coupling = jnp.where(inside[:, None], bus_coupling[clipped], jnp.zeros_like(bus_coupling))
        weight = tie_admittance[:, column][:, None] * bus_coupling * far_coupling
        tie_term = weight[None] * (input_vector - input_vector[:, clipped])
        summed = summed + tie_term
        summed = summed.at[:, clipped].add(-tie_term)
    return summed


def security_product(input_vector, con_sens, con_weight, con_owner):
    blocks = con_sens.shape[0] // NCON_DEV
    sensitivity_blocks = con_sens.reshape(blocks, NCON_DEV, con_sens.shape[1])
    weight_tiles = con_weight.reshape(blocks, NCON_DEV, con_weight.shape[1])
    owner_blocks = con_owner[:, 0].astype(jnp.int32).reshape(blocks, NCON_DEV)

    def visit_block(summed, block_items):
        sensitivity, weight, owner_area = block_items
        chosen_entries = input_vector[:, owner_area, :]
        flows = jnp.einsum('tcb,cb->tc', chosen_entries, sensitivity, precision=lax.Precision.HIGHEST)
        scaled = flows * weight.T
        summed = summed.at[:, owner_area, :].add(scaled[:, :, None] * sensitivity[None])
        return summed, None

    summed, unused = lax.scan(visit_block, jnp.zeros_like(input_vector), (sensitivity_blocks, weight_tiles, owner_blocks))
    return summed


def apply_operator(input_vector, diagonal_entries, tile, ramp_weight, bus_coupling, tie_offset, tie_admittance, con_sens, con_weight, con_owner):
    operator_output = diagonal_entries * input_vector + jnp.einsum('uog,ogn->uon', input_vector, tile, precision=lax.Precision.HIGHEST)
    padded = jnp.pad(input_vector, ((1, 1), (0, 0), (0, 0)))
    operator_output = operator_output + ramp_weight[None] * (2.0 * input_vector - padded[:-2] - padded[2:])
    operator_output = operator_output + tie_product(input_vector, bus_coupling, tie_offset, tie_admittance)
    return operator_output + security_product(input_vector, con_sens, con_weight, con_owner)


def reference(gradient, barrier, slack, hess_diag, tile, ramp_weight, bus_coupling, tie_offset, tie_admittance, con_sens, con_weight, con_owner, step_guess):
    diagonal_entries = hess_diag + barrier[0] / (slack * slack)
    right_side = barrier[0] / slack - gradient

    def operate(input_vector):
        return apply_operator(input_vector, diagonal_entries, tile, ramp_weight, bus_coupling, tie_offset, tie_admittance, con_sens, con_weight, con_owner)

    solution = step_guess
    residual = right_side - operate(solution)
    search_direction = residual
    norm_now = jnp.sum(residual * residual)
    for iteration in range(ITERS):
        applied = operate(search_direction)
        step_size = norm_now / jnp.sum(search_direction * applied)
        solution = solution + step_size * search_direction
        residual = residual - step_size * applied
        if iteration + 1 < ITERS:
            norm_next = jnp.sum(residual * residual)
            search_direction = residual + (norm_next / norm_now) * search_direction
            norm_now = norm_next
    return solution, residual
```

```python
import functools
import jax
import jax.numpy as jnp
from jax import lax
from jax.experimental import pallas as pl
from jax.experimental.pallas import tpu as pltpu
from jax.sharding import PartitionSpec as P

TIES = 4
HOUR_LANES = 64
F32 = jnp.float32
BF16 = jnp.bfloat16
VMEM_LIMIT = 40 * 1024 * 1024

WHOLE = pl.BlockSpec(memory_space=pltpu.VMEM)
SCALARS = pl.BlockSpec(memory_space=pltpu.SMEM)


def call(kernel, out_shape, in_specs, flops, moved, scratch=()):
    many = isinstance(out_shape, (tuple, list))
    return pl.pallas_call(
        kernel,
        out_shape=out_shape,
        in_specs=in_specs,
        out_specs=jax.tree.map(lambda _: WHOLE, out_shape) if many else WHOLE,
        scratch_shapes=scratch,
        compiler_params=pltpu.CompilerParams(vmem_limit_bytes=VMEM_LIMIT),
        cost_estimate=pl.CostEstimate(flops=flops, bytes_accessed=moved, transcendentals=0),
    )


def f32_shape(*shape):
    return jax.ShapeDtypeStruct(shape, F32)


def two_parts(value):
    high = value.astype(BF16)
    return high, (value - high.astype(F32)).astype(BF16)


def three_parts(value):
    high = value.astype(BF16)
    rest = value - high.astype(F32)
    middle = rest.astype(BF16)
    return high, middle, (rest - middle.astype(F32)).astype(BF16)


def dot(left, right, contract_right=0):
    return lax.dot_general(
        left, right, (((1,), (contract_right,)), ((), ())), preferred_element_type=F32
    )


def split_dot(left, right_high, right_low, contract_right=0):
    high, low = two_parts(left)
    return (
        dot(high, right_high, contract_right)
        + dot(low, right_high, contract_right)
        + dot(high, right_low, contract_right)
    )


def pack_kernel(span, cap, index, owner, sens, weight, sens_out, weight_out):
    rows = owner.shape[0]
    groups = sens_out.shape[0] // cap
    owner_column = owner[...].astype(F32)
    wide = jnp.broadcast_to(owner_column, (rows, 128))
    owner_row = jnp.transpose(wide)[0:1, :]
    earlier = lax.broadcasted_iota(jnp.int32, (rows, rows), 0) < lax.broadcasted_iota(
        jnp.int32, (rows, rows), 1
    )
    same = jnp.where(earlier & (owner_column == owner_row), 1.0, 0.0)
    rank_row = jnp.sum(same, axis=0, keepdims=True)
    key_row = owner_row * cap + rank_row
    slots = groups * cap
    slot = lax.broadcasted_iota(jnp.int32, (slots, rows), 0)
    group, rank = slot // cap, slot % cap

    def marks(area):
        wanted = ((group * span + area) * cap + rank).astype(F32)
        return jnp.where(wanted == key_row, 1.0, 0.0).astype(BF16)

    mine = marks(index[0])
    high, middle, low = three_parts(sens[...])
    sens_out[...] = (dot(mine, high) + dot(mine, middle)) + dot(mine, low)
    hours = weight.shape[1]
    gap = jnp.zeros((rows, HOUR_LANES - hours), F32)
    blank = jnp.zeros((rows, HOUR_LANES), F32)
    left = jnp.concatenate([weight[...], gap, blank], axis=1)
    right = jnp.concatenate([blank, weight[...], gap], axis=1)
    left_parts, right_parts = three_parts(left), three_parts(right)
    for pair in range(span // 2):
        first, second = marks(2 * pair), marks(2 * pair + 1)
        total = None
        for a, b in zip(left_parts, right_parts):
            term = dot(first, a) + dot(second, b)
            total = term if total is None else total + term
        weight_out[:, pl.ds(128 * pair, 128)] = total


def take(ref, area, span):
    rows = pl.ds(area, ref.shape[1] // span, stride=span)
    return jnp.concatenate([ref[k, rows, :] for k in range(ref.shape[0])], axis=1)


def put(ref, area, span, value):
    rows = pl.ds(area, ref.shape[1] // span, stride=span)
    for k in range(ref.shape[0]):
        ref[k, rows, :] = value[:, 128 * k : 128 * (k + 1)]


def ties_from(coefficients, fields, couplings):
    total = None
    for coefficient, field, coupling in zip(coefficients, fields, couplings):
        term = coefficient * (coupling * field)
        total = term if total is None else total + term
    return total


def upper(ties, span, i, j):
    return ties[span + i, j + span - i - 1] if j <= i else 0.0


def lower(ties, span, i, j):
    return ties[j, i + span - j - 1] if j >= i else 0.0


def local_tie(ties, span, i, j):
    a, b = min(i, j), max(i, j)
    return ties[span + a, b - a - 1]


def cross_coefficients(ties, odd, span, i):
    near, far = [], []
    for j in range(span):
        up, down = upper(ties, span, i, j), lower(ties, span, i, j)
        near.append(jnp.where(odd, down, up))
        far.append(jnp.where(odd, up, down))
    return near, far


def halo_terms(ramp, before, after, target, sign):
    span = ramp.shape[0]
    blocks, rows = target.shape[:2]
    for k in range(blocks):
        weight = sign * ramp[:, 128 * k : 128 * (k + 1)]
        target[k, 0:span, :] = target[k, 0:span, :] - weight * before[k]
        target[k, rows - span : rows, :] = target[k, rows - span : rows, :] - weight * after[k]


def interior_ramp(ramp, field, target, span):
    hours = field.shape[1] // span
    for i in range(span):
        own = take(field, i, span)
        blank = jnp.zeros((1, own.shape[1]), F32)
        neighbours = jnp.concatenate([blank, own[: hours - 1]], axis=0) + jnp.concatenate(
            [own[1:], blank], axis=0
        )
        target[i] = ramp[i : i + 1, :] * neighbours


def first_kernel(
    span,
    index,
    ties,
    guess,
    right_side,
    diagonal_in,
    tile,
    ramp,
    coupling,
    near,
    far,
    near_coupling,
    far_coupling,
    before,
    after,
    partial,
    diagonal,
    tile_high,
    tile_low,
    ramped,
):
    odd = index[1] == 1
    interior_ramp(ramp, guess, ramped, span)
    for i in range(span):
        high, low = two_parts(tile[i])
        tile_high[i] = high
        tile_low[i] = low
        own = take(guess, i, span)
        own_coupling = coupling[i : i + 1, :]
        near_of, far_of = cross_coefficients(ties, odd, span, i)
        others = [j for j in range(span) if j != i]
        strength = jnp.zeros_like(own_coupling)
        pull = jnp.zeros_like(own)
        for j in others:
            w = local_tie(ties, span, i, j)
            strength = strength + w * coupling[j : j + 1, :]
            pull = pull + w * (coupling[j : j + 1, :] * take(guess, j, span))
        for j in range(span):
            strength = strength + near_of[j] * near_coupling[j : j + 1, :]
            strength = strength + far_of[j] * far_coupling[j : j + 1, :]
            pull = pull + near_of[j] * (near_coupling[j : j + 1, :] * take(near, j, span))
            pull = pull + far_of[j] * (far_coupling[j : j + 1, :] * take(far, j, span))
        folded = take(diagonal_in, i, span) + (
            2.0 * ramp[i : i + 1, :] + own_coupling * strength
        )
        put(diagonal, i, span, folded)
        image = folded * own + split_dot(own, high, low) - ramped[i] - own_coupling * pull
        put(partial, i, span, take(right_side, i, span) - image)
    halo_terms(ramp, before, after, partial, -1.0)


def security(own, high, low, weight):
    flows = split_dot(own, high, low, 1)
    return split_dot(flows * weight, high, low)


def owned_kernel(span, index, guess, partial, weights, *refs):
    pieces, (residual, high_out, low_out, weight_out) = refs[:span], refs[span:]
    hours = guess.shape[1] // span
    for pair in range(span // 2):
        turned = jnp.transpose(weights[:, pl.ds(128 * pair, 128)])
        weight_out[2 * pair] = turned[:hours]
        weight_out[2 * pair + 1] = turned[HOUR_LANES : HOUR_LANES + hours]
    for step in range(span):
        area = index[0] ^ step
        high, low = two_parts(pieces[step][...])
        high_out[step] = high
        low_out[step] = low
        term = security(take(guess, area, span), high, low, weight_out[area])
        put(residual, area, span, take(partial, area, span) - term)


def local_kernel(
    span,
    with_sums,
    index,
    ties,
    field,
    diagonal,
    ramp,
    coupling,
    tile_high,
    tile_low,
    sens_high,
    sens_low,
    weights,
    *refs,
):
    if with_sums:
        earlier, image, sums, ramped = refs
    else:
        image, ramped = refs
    interior_ramp(ramp, field, ramped, span)
    for i in range(span):
        own = take(field, i, span)
        pull = jnp.zeros_like(own)
        for j in range(span):
            if j != i:
                pull = pull + local_tie(ties, span, i, j) * (
                    coupling[j : j + 1, :] * take(field, j, span)
                )
        value = (
            take(diagonal, i, span) * own
            + split_dot(own, tile_high[i], tile_low[i])
            - ramped[i]
            - coupling[i : i + 1, :] * pull
        )
        put(image, i, span, value)
    for step in range(span):
        area = index[0] ^ step
        term = security(
            take(field, area, span), sens_high[step], sens_low[step], weights[area]
        )
        put(image, area, span, take(image, area, span) + term)
    if with_sums:
        a, b = earlier[...], field[...]
        sums[...] = lanes_of([jnp.sum(a * a), jnp.sum(a * b), jnp.sum(b * b)])


def lanes_of(values):
    lane = lax.broadcasted_iota(jnp.int32, (1, 128), 1)
    row = jnp.zeros((1, 128), F32)
    for position, value in enumerate(values):
        row = jnp.where(lane == position, value, row)
    return row


def cross_kernel(
    span,
    with_sums,
    index,
    ties,
    image,
    near,
    far,
    near_coupling,
    far_coupling,
    before,
    after,
    ramp,
    coupling,
    *refs,
):
    if with_sums:
        earlier, sums, total, spread = refs
    else:
        (total,) = refs
    odd = index[1] == 1
    near_fields = [near_coupling[j : j + 1, :] * take(near, j, span) for j in range(span)]
    far_fields = [far_coupling[j : j + 1, :] * take(far, j, span) for j in range(span)]
    for i in range(span):
        near_of, far_of = cross_coefficients(ties, odd, span, i)
        pull = near_of[0] * near_fields[0] + far_of[0] * far_fields[0]
        for j in range(1, span):
            pull = pull + near_of[j] * near_fields[j] + far_of[j] * far_fields[j]
        put(total, i, span, take(image, i, span) - coupling[i : i + 1, :] * pull)
    halo_terms(ramp, before, after, total, 1.0)
    if with_sums:
        last = jnp.sum(earlier[...] * total[...])
        lane = lax.broadcasted_iota(jnp.int32, (1, 128), 1)
        spread[...] = jnp.broadcast_to(jnp.where(lane == 3, last, sums[...]), spread.shape)


def last_kernel(gathered, guess, residual, image, second, step_out, residual_out):
    sums = jnp.sum(gathered[...], axis=0, keepdims=True)
    rr, ra, aa, ab = (sums[:, k : k + 1] for k in range(4))
    alpha = rr / ra
    rr_next = alpha * (alpha * aa - ra)
    beta = rr_next / rr
    product = ra - 2.0 * alpha * aa + alpha * alpha * ab
    alpha_next = rr_next / (product - beta * rr_next / alpha)
    one = alpha + alpha_next * (1.0 + beta)
    two = alpha_next * alpha
    hours, span, width = step_out.shape
    for k in range(width // 128):
        lanes = pl.ds(128 * k, 128)
        step = guess[k] + one * residual[k] - two * image[k]
        left = residual[k] - one * image[k] + two * second[k]
        step_out[:, :, lanes] = step.reshape(hours, span, 128)
        residual_out[:, :, lanes] = left.reshape(hours, span, 128)


def exchange(field, groups):
    far_pairs = [(i, i + 1) for i in range(1, groups - 1, 2)]
    far = lax.ppermute(field, "area", far_pairs + [(j, i) for i, j in far_pairs])
    near = lax.ppermute(field, "area", [(i, i ^ 1) for i in range(groups)])
    return near, far


def hour_halo(field, span):
    count = lax.axis_size("tm")
    rows = field.shape[1]
    up = [(i, i + 1) for i in range(count - 1)]
    before = lax.ppermute(field[:, rows - span :], "tm", up)
    after = lax.ppermute(field[:, :span], "tm", [(j, i) for i, j in up])
    return before, after


def body(
    gradient,
    barrier,
    slack,
    hess_diag,
    tile,
    ramp_weight,
    bus_coupling,
    tie_offset,
    tie_admittance,
    con_sens,
    con_weight,
    con_owner,
    step_guess,
):
    hours, span, width = gradient.shape
    total_areas = tie_offset.shape[0]
    groups, members = lax.axis_size("area"), lax.axis_size("tm")
    assert members == span and members & (members - 1) == 0 and hours <= HOUR_LANES
    rows_held = con_sens.shape[0]
    cap = max(2, (2 * rows_held + total_areas - 1) // total_areas)
    slots = groups * cap
    rows = hours * span
    member, group = lax.axis_index("tm"), lax.axis_index("area")
    index = jnp.stack([member, group % 2]).astype(jnp.int32)

    sens_send, weight_send = call(
        functools.partial(pack_kernel, span, cap),
        (f32_shape(slots, width), f32_shape(slots, span * HOUR_LANES)),
        [SCALARS, WHOLE, WHOLE, WHOLE],
        6 * slots * rows_held * width,
        4 * rows_held * width * 2,
    )(index, con_owner, con_sens, con_weight)
    piece = lax.all_to_all(
        sens_send.reshape(groups, cap, width), "area", split_axis=0, concat_axis=0, tiled=True
    )
    weights = lax.all_to_all(
        weight_send.reshape(groups, cap, span * HOUR_LANES),
        "area",
        split_axis=0,
        concat_axis=0,
        tiled=True,
    ).reshape(slots, span * HOUR_LANES)
    piece = piece.reshape(slots, width)
    pieces = [piece] + [
        lax.ppermute(piece, "tm", [(i, i ^ step) for i in range(members)])
        for step in range(1, members)
    ]

    padded = (jnp.pad(tie_offset, ((span, 0), (0, 0))), jnp.pad(tie_admittance, ((span, 0), (0, 0))))
    offsets, gains = (
        lax.dynamic_slice(a, (group * span, jnp.int32(0)), (2 * span, TIES)) for a in padded
    )
    steps_up = jnp.arange(1, span + 1, dtype=jnp.int32)
    ties = jnp.sum(
        jnp.where(offsets[:, :, None] == steps_up[None, None, :], gains[:, :, None], 0.0), axis=1
    )

    def blocked(value):
        return jnp.swapaxes(value.reshape(rows, width // 128, 128), 0, 1)

    guess = blocked(step_guess)
    diagonal_in = blocked(hess_diag + barrier[0] / (slack * slack))
    right_side = blocked(barrier[0] / slack - gradient)
    near_guess, far_guess = exchange(guess, groups)
    near_coupling, far_coupling = exchange(bus_coupling, groups)
    before, after = hour_halo(guess, span)
    ramped = [pltpu.VMEM((span, hours, width), F32)]
    field_shape = f32_shape(width // 128, rows, 128)
    tile_shape = jax.ShapeDtypeStruct(tile.shape, BF16)
    tile_flops = 6 * rows * width * width
    partial, diagonal, tile_high, tile_low = call(
        functools.partial(first_kernel, span),
        (field_shape, field_shape, tile_shape, tile_shape),
        [SCALARS, SCALARS] + [WHOLE] * 12,
        tile_flops,
        8 * span * width * width,
        ramped,
    )(
        index,
        ties,
        guess,
        right_side,
        diagonal_in,
        tile,
        ramp_weight,
        bus_coupling,
        near_guess,
        far_guess,
        near_coupling,
        far_coupling,
        before,
        after,
    )

    sens_shape = jax.ShapeDtypeStruct((span, slots, width), BF16)
    residual, sens_high, sens_low, owned_weight = call(
        functools.partial(owned_kernel, span),
        (field_shape, sens_shape, sens_shape, f32_shape(span, hours, slots)),
        [SCALARS] + [WHOLE] * (3 + span),
        12 * rows * slots * width,
        6 * span * slots * width,
    )(index, guess, partial, weights, *pieces)

    def apply(field, earlier=None):
        near, far = exchange(field, groups)
        before, after = hour_halo(field, span)
        summed = earlier is not None
        image = call(
            functools.partial(local_kernel, span, summed),
            (field_shape, f32_shape(1, 128)) if summed else field_shape,
            [SCALARS, SCALARS] + [WHOLE] * (9 + summed),
            tile_flops + 12 * rows * slots * width,
            4 * span * width * width,
            ramped,
        )(
            index,
            ties,
            field,
            diagonal,
            ramp_weight,
            bus_coupling,
            tile_high,
            tile_low,
            sens_high,
            sens_low,
            owned_weight,
            *([earlier] if summed else []),
        )
        more = ()
        if summed:
            image, sums = image
            more = (field, sums)
        return call(
            functools.partial(cross_kernel, span, summed),
            (field_shape, f32_shape(groups * members, 128)) if summed else field_shape,
            [SCALARS, SCALARS] + [WHOLE] * (9 + len(more)),
            64 * rows * width,
            16 * rows * width,
        )(
            index,
            ties,
            image,
            near,
            far,
            near_coupling,
            far_coupling,
            before,
            after,
            ramp_weight,
            bus_coupling,
            *more,
        )

    image = apply(residual)
    second, spread = apply(image, residual)
    gathered = lax.all_to_all(spread, ("tm", "area"), split_axis=0, concat_axis=0, tiled=True)
    out_shape = f32_shape(hours, span, width)
    return call(
        last_kernel,
        (out_shape, out_shape),
        [WHOLE] * 5,
        8 * rows * width,
        24 * rows * width,
    )(gathered, guess, residual, image, second)


def solution(mesh):
    field = P("tm", "area", None)
    placed = (
        field,
        P(),
        field,
        field,
        P("area", None, None),
        P("area", None),
        P("area", None),
        P(),
        P(),
        P("area", None),
        P("area", "tm"),
        P("area", None),
        field,
    )
    return jax.shard_map(
        body, mesh=mesh, in_specs=placed, out_specs=(field, field), check_vma=False
    )
```

```python
import functools
import jax
import jax.numpy as jnp
from jax import lax
from jax.experimental import pallas as pl
from jax.experimental.pallas import tpu as pltpu
from jax.sharding import PartitionSpec as P

TIES = 4
HOUR_LANES = 64
LANES = 128
FIRST = 10**10
WIDE = 256
F32 = jnp.float32
BF16 = jnp.bfloat16
VMEM_LIMIT = 12 * 1024 * 1024

WHOLE = pl.BlockSpec(memory_space=pltpu.VMEM)
SCALARS = pl.BlockSpec(memory_space=pltpu.SMEM)
UNREAD = pl.BlockSpec(memory_space=pl.ANY)
IN_HBM = pl.BlockSpec(memory_space=pltpu.HBM)


def call(kernel, out_shape, in_specs, scratch=(), flops=1, out_specs=None):
    many = isinstance(out_shape, (tuple, list))
    if out_specs is None:
        out_specs = [WHOLE] * len(out_shape) if many else WHOLE
    inner = getattr(kernel, "func", kernel)
    return pl.pallas_call(
        kernel,
        name=inner.__name__,
        out_shape=out_shape,
        in_specs=in_specs,
        out_specs=out_specs,
        scratch_shapes=scratch,
        compiler_params=pltpu.CompilerParams(vmem_limit_bytes=VMEM_LIMIT),
        cost_estimate=pl.CostEstimate(flops=flops, bytes_accessed=1, transcendentals=0),
    )


def landing(*operands):
    return [pltpu.VMEM(a.shape, a.dtype) for a in operands] + [
        pltpu.SemaphoreType.DMA((len(operands),))
    ]


def in_hbm(*operands):
    return [pltpu.with_memory_space_constraint(a, pltpu.HBM) for a in operands]


def fetch(sources, targets, semaphores):
    copies = [
        pltpu.make_async_copy(source, target, semaphores.at[k])
        for k, (source, target) in enumerate(zip(sources, targets))
    ]
    for copy in copies:
        copy.start()
    return copies


def f32_shape(*shape):
    return jax.ShapeDtypeStruct(shape, F32)


def two_parts(value):
    high = value.astype(BF16)
    return high, (value - high.astype(F32)).astype(BF16)


def three_parts(value):
    high = value.astype(BF16)
    rest = value - high.astype(F32)
    middle = rest.astype(BF16)
    return high, middle, (rest - middle.astype(F32)).astype(BF16)


def dot(left, right, contract_right=0):
    return lax.dot_general(
        left, right, (((1,), (contract_right,)), ((), ())), preferred_element_type=F32
    )


def split_dot(left, right_high, right_low, contract_right=0):
    high, low = two_parts(left)
    return (
        dot(high, right_high, contract_right)
        + dot(low, right_high, contract_right)
        + dot(high, right_low, contract_right)
    )


def take(ref, area, span, first=0, hours=None):
    hours = ref.shape[1] // span - first if hours is None else hours
    rows = pl.ds(area + span * first, hours, stride=span)
    return jnp.concatenate([ref[k, rows, :] for k in range(ref.shape[0])], axis=1)


def put(ref, area, span, value):
    rows = pl.ds(area, value.shape[0], stride=span)
    for k in range(ref.shape[0]):
        ref[k, rows, :] = value[:, LANES * k : LANES * (k + 1)]


def row_of(ref, row):
    return jnp.concatenate([ref[k, row : row + 1, :] for k in range(ref.shape[0])], axis=1)


def keys_of(owner, cap):
    rows = owner.shape[1]
    owner_row = owner[...].astype(F32)
    owner_column = jnp.transpose(jnp.broadcast_to(owner_row, (LANES, rows)))[:, 0:1]
    earlier = lax.broadcasted_iota(jnp.int32, (rows, rows), 0) < lax.broadcasted_iota(
        jnp.int32, (rows, rows), 1
    )
    same = jnp.where(earlier & (owner_column == owner_row), 1.0, 0.0)
    return owner_row * cap + jnp.sum(same, axis=0, keepdims=True)


def marks_of(keys, area, rank, cap):
    return jnp.where((area * cap + rank).astype(F32) == keys, 1.0, 0.0).astype(BF16)


def pack_kernel(span, cap, hours, index, owner_far, sens_far, weight_far, *outs):
    *away, here, other, owner, sens, weight, semaphores = outs
    copies = fetch((owner_far, sens_far, weight_far), (owner, sens, weight), semaphores)
    chip, core, member = index[0], index[1], index[2]
    blocks = owner.shape[1]
    parts = sens.shape[1] // WIDE
    copies[0].wait()
    keys = keys_of(owner, cap)
    slot = lax.broadcasted_iota(jnp.int32, (2 * cap * (len(away) + 1), blocks), 0)
    group = (chip ^ (slot // (2 * cap))) * 2 + (core ^ (slot // cap % 2))
    local = lax.broadcasted_iota(jnp.int32, (2 * span * cap, blocks), 0)
    local_group = chip * 2 + (core ^ (local // (span * cap)))
    local_area = local_group * span + (member ^ (local // cap % span))
    sens_marks = jnp.concatenate(
        [
            marks_of(keys, group * span + member, slot % cap, cap)[2 * cap :],
            marks_of(keys, local_area, local % cap, cap),
        ],
        axis=0,
    )
    area_marks = [marks_of(keys, group * span + k, slot % cap, cap) for k in range(span)]
    copies[2].wait()
    gap = jnp.zeros((LANES - hours, blocks), F32)
    by_block = jnp.transpose(jnp.concatenate([weight[...], gap], axis=0))
    left_parts = two_parts(by_block)
    right_parts = two_parts(pltpu.roll(by_block, HOUR_LANES, 1))
    weights = jnp.concatenate(
        [
            sum(
                dot(area_marks[2 * pair], a) + dot(area_marks[2 * pair + 1], b)
                for a, b in zip(left_parts, right_parts)
            )
            for pair in range(span // 2)
        ],
        axis=1,
    )
    copies[1].wait()
    high, low = two_parts(sens[...])
    rows = dot(sens_marks, high) + dot(sens_marks, low)
    for k in range(len(away)):
        for core_step in range(2):
            row, at = cap * (2 * k + core_step), cap * (parts + 1) * core_step
            for part in range(parts):
                lanes = slice(WIDE * part, WIDE * (part + 1))
                away[k][pl.ds(at + cap * part, cap), :] = rows[row : row + cap, lanes]
            away[k][pl.ds(at + cap * parts, cap), :] = weights[2 * cap + row :][:cap]
    count = span * cap
    for core_step, out in ((0, here), (1, other)):
        row = 2 * cap * len(away) + count * core_step
        for part in range(parts):
            lanes = slice(WIDE * part, WIDE * (part + 1))
            out[pl.ds(count * part, count), :] = rows[row : row + count, lanes]
        out[pl.ds(count * parts, cap), :] = weights[cap * core_step :][:cap]


def fields_kernel(barrier, *refs):
    guess_out, right_out, diagonal_out = refs[-9:-6]
    guess, gradient, slack, hess, coupling, semaphores = landed = refs[-6:]
    for copy in fetch(refs[:5], landed[:5], semaphores):
        copy.wait()
    hours, span, width = guess.shape
    rows = hours * span
    shape = (rows, LANES)
    for k in range(width // LANES):
        lanes = pl.ds(LANES * k, LANES)
        slack_rows = slack[:, :, lanes].reshape(shape)
        guess_out[k, pl.ds(0, rows), :] = guess[:, :, lanes].reshape(shape)
        guess_out[k, pl.ds(rows, span), :] = coupling[:, LANES * k : LANES * (k + 1)]
        guess_out[k, pl.ds(rows + span, span), :] = jnp.zeros((span, LANES), F32)
        right_out[k] = barrier[0] / slack_rows - gradient[:, :, lanes].reshape(shape)
        diagonal_out[k] = hess[:, :, lanes].reshape(shape) + barrier[0] / (
            slack_rows * slack_rows
        )


def halves_kernel(index, tile_far, offsets_far, gains_far, after, *refs):
    tile_high, tile_low, ties, offsets, gains, tile, semaphores = refs
    span = tile.shape[0]
    each = [tile_far.at[i] for i in range(span)]
    copies = fetch(
        [offsets_far, gains_far] + each,
        [offsets, gains] + [tile.at[i] for i in range(span)],
        semaphores,
    )
    copies[0].wait()
    copies[1].wait()
    first = (index[0] * 2 + index[1] - 1) * span
    for i in range(2 * span):
        area = jnp.maximum(first + i, 0)
        for step in range(span):
            total = 0.0
            for k in range(offsets.shape[0]):
                total = total + jnp.where(offsets[k, area] == step + 1, gains[k, area], 0.0)
            ties[i, step] = total
    for i in range(span):
        copies[2 + i].wait()
        high, low = two_parts(tile[i])
        tile_high[i] = high
        tile_low[i] = low


def weights_kernel(span, cap, here, beside, crossed, *refs):
    *arrived, weights = refs
    hours = weights.shape[1]
    chunk = arrived[0].shape[0] // 2
    pieces = [ref[pl.ds(ref.shape[0] - cap, cap), :] for ref in (here, beside)]
    for k, ref in enumerate(arrived):
        pieces.append(ref[pl.ds(chunk - cap, cap), :])
        pieces.append(crossed[pl.ds(chunk * (k + 1) - cap, cap), :])
    by_slot = jnp.concatenate(pieces, axis=0)
    for pair in range(span // 2):
        turned = jnp.transpose(by_slot[:, LANES * pair : LANES * (pair + 1)])
        for half in range(2):
            weights[2 * pair + half] = turned[HOUR_LANES * half :][:hours]


def upper(ties, span, i, j):
    return ties[span + i, j + span - i - 1] if j <= i else 0.0


def lower(ties, span, i, j):
    return ties[j, i + span - j - 1] if j >= i else 0.0


def local_tie(ties, span, i, j):
    a, b = min(i, j), max(i, j)
    return ties[span + a, b - a - 1]


def cross_coefficients(ties, odd, span, i):
    near, far = [], []
    for j in range(span):
        up, down = upper(ties, span, i, j), lower(ties, span, i, j)
        near.append(jnp.where(odd, down, up))
        far.append(jnp.where(odd, up, down))
    return near, far


def both_hours(field, area, span, hours):
    return take(field, area, span, 0, hours) + take(field, area, span, 2, hours)


def both_hours_inside(own):
    blank = jnp.zeros((1, own.shape[1]), F32)
    earlier = jnp.concatenate([blank, own[: own.shape[0] - 1]], axis=0)
    return earlier + jnp.concatenate([own[1:], blank], axis=0)


def local_pull(ties, coupling, field, span, i, hours, first=1):
    pull = None
    for j in range(span):
        if j != i:
            term = local_tie(ties, span, i, j) * (
                coupling[j : j + 1, :] * take(field, j, span, first, hours)
            )
            pull = term if pull is None else pull + term
    return pull


def first_kernel(
    span,
    deep,
    index,
    ties,
    guess,
    right,
    diagonal_in,
    near,
    far,
    weights,
    tile_high,
    tile_low,
    ramp,
    coupling,
    partial,
    diagonal,
    up,
    down,
):
    odd = index[1] == 1
    blocks, rows = right.shape[:2]
    hours = rows // span
    near_coupling = [row_of(near, rows + j) for j in range(span)]
    far_coupling = [row_of(far, rows + j) for j in range(span)]
    near_fields = [near_coupling[j] * take(near, j, span, 0, hours) for j in range(span)]
    far_fields = [far_coupling[j] * take(far, j, span, 0, hours) for j in range(span)]
    for i in range(span):
        own = take(guess, i, span, 0, hours)
        own_coupling = coupling[i : i + 1, :]
        own_ramp = ramp[i : i + 1, :]
        near_of, far_of = cross_coefficients(ties, odd, span, i)
        strength = jnp.zeros_like(own_coupling)
        pull = local_pull(ties, coupling, guess, span, i, hours, 0)
        for j in range(span):
            if j != i:
                strength = strength + local_tie(ties, span, i, j) * coupling[j : j + 1, :]
            strength = strength + near_of[j] * near_coupling[j] + far_of[j] * far_coupling[j]
            pull = pull + near_of[j] * near_fields[j] + far_of[j] * far_fields[j]
        folded = take(diagonal_in, i, span) + (2.0 * own_ramp + own_coupling * strength)
        put(diagonal, i, span, folded)
        image = (
            folded * own
            + split_dot(own, tile_high[i], tile_low[i])
            - own_ramp * both_hours_inside(own)
            - own_coupling * pull
        )
        put(partial, i, span, take(right, i, span) - image)
    for k in range(blocks):
        for out, low in ((up, False), (down, True)):
            at = 0
            for source, count in (
                (partial, deep * span),
                (guess, deep * span),
                (diagonal, (deep - 1) * span),
            ):
                start = 0 if low else rows - count
                out[k, pl.ds(at, count), :] = source[k, pl.ds(start, count), :]
                at += count
            start = 0 if low else hours - deep
            out[k, pl.ds(at, deep), :] = weights[k, pl.ds(start, deep), :]
            out[k, pl.ds(at + deep, deep), :] = jnp.zeros((deep, LANES), F32)


def security(own, high, low, weight):
    flows = split_dot(own, high, low, 1)
    return split_dot(flows * weight, high, low)


def clear_outside(index, target, count):
    blocks, rows = target.shape[:2]
    keep_first = jnp.where(index[2] == 0, 0.0, 1.0)
    keep_last = jnp.where(index[2] == index[3] - 1, 0.0, 1.0)
    for k in range(blocks):
        target[k, 0:count, :] = target[k, 0:count, :] * keep_first
        target[k, rows - count : rows, :] = target[k, rows - count : rows, :] * keep_last


def owned_kernel(
    span,
    cap,
    deep,
    index,
    guess_in,
    partial_in,
    diagonal_in,
    weights_in,
    before,
    after,
    ramp,
    here,
    beside,
    *refs,
):
    pieces, outs = refs[:span], refs[span:]
    residual, sent, high_out, low_out, diagonal, weights, guess, partial = outs
    blocks, rows = partial_in.shape[:2]
    for k in range(blocks):
        at = 0
        for target, middle, edge in (
            (partial, partial_in, deep * span),
            (guess, guess_in, deep * span),
            (diagonal, diagonal_in, (deep - 1) * span),
        ):
            target[k, pl.ds(0, edge), :] = before[k, pl.ds(at, edge), :]
            target[k, pl.ds(edge, rows), :] = middle[k, pl.ds(0, rows), :]
            target[k, pl.ds(edge + rows, edge), :] = after[k, pl.ds(at, edge), :]
            at += edge
        edge = ramp[:, LANES * k : LANES * (k + 1)]
        for hour, other in (
            (deep - 1, deep),
            (deep, deep - 1),
            (rows // span + deep - 1, rows // span + deep),
            (rows // span + deep, rows // span + deep - 1),
        ):
            target = pl.ds(span * hour, span)
            partial[k, target, :] = (
                partial[k, target, :] + edge * guess[k, pl.ds(span * other, span), :]
            )
    for area in range(span):
        weights[area] = jnp.concatenate(
            [before[area, pl.ds(at, deep), :], weights_in[area], after[area, pl.ds(at, deep), :]],
            axis=0,
        )
    parts = guess.shape[0] * LANES // WIDE
    group = pieces[0].shape[0] // (parts * cap)
    terms = []
    for step in range(span):
        area = index[2] ^ step
        wide = []
        for part in range(parts):
            at = cap * (span * part + step)
            rows = [here[pl.ds(at, cap), :], beside[pl.ds(at, cap), :]]
            rows += [
                pieces[step][pl.ds(cap * (parts * k + part), cap), :] for k in range(group)
            ]
            wide.append(jnp.concatenate(rows, axis=0))
        high, low = two_parts(jnp.concatenate(wide, axis=1))
        high_out[step] = high
        low_out[step] = low
        term = security(take(guess, area, span), high, low, weights[area])
        terms.append(take(partial, area, span) - term)
    for step in range(span):
        put(residual, index[2] ^ step, span, terms[step])
    clear_outside(index, residual, deep * span)
    for k in range(sent.shape[0]):
        sent[k] = residual[k, pl.ds(span, sent.shape[1]), :]


def local_kernel(
    span,
    skip,
    with_sums,
    index,
    ties,
    field,
    diagonal,
    ramp,
    coupling,
    tile_high,
    tile_low,
    sens_high,
    sens_low,
    weights,
    *refs,
):
    if with_sums:
        earlier, image, sums = refs
    else:
        (image,) = refs
    hours = image.shape[1] // span
    for i in range(span):
        value = (
            take(diagonal, i, span, skip - 1, hours) * take(field, i, span, 1, hours)
            + split_dot(take(field, i, span, 1, hours), tile_high[i], tile_low[i])
            - ramp[i : i + 1, :] * both_hours(field, i, span, hours)
            - coupling[i : i + 1, :] * local_pull(ties, coupling, field, span, i, hours)
        )
        put(image, i, span, value)
    terms = []
    for step in range(span):
        area = index[2] ^ step
        weight = weights[area][skip : skip + hours]
        own = take(field, area, span, 1, hours)
        terms.append(security(own, sens_high[step], sens_low[step], weight))
    for step in range(span):
        area = index[2] ^ step
        put(image, area, span, take(image, area, span) + terms[step])
    if with_sums:
        count = image.shape[1]
        first = (earlier.shape[1] - count) // 2
        a, b = earlier[:, pl.ds(first, count), :], field[:, pl.ds(span, count), :]
        sums[...] = lanes_of([jnp.sum(a * a), jnp.sum(a * b), jnp.sum(b * b)])


def lanes_of(values):
    lane = lax.broadcasted_iota(jnp.int32, (1, LANES), 1)
    row = jnp.zeros((1, LANES), F32)
    for position, value in enumerate(values):
        row = jnp.where(lane == position, value, row)
    return row


def cross_kernel(
    span, with_sums, index, ties, image, near, far, near_first, far_first, coupling, *refs
):
    if with_sums:
        earlier, sums, total, spread = refs
    else:
        total, sent = refs
    odd = index[1] == 1
    hours = image.shape[1] // span
    count = near_first.shape[1] - 2 * span
    near_fields = [row_of(near_first, count + j) * take(near, j, span) for j in range(span)]
    far_fields = [row_of(far_first, count + j) * take(far, j, span) for j in range(span)]
    for i in range(span):
        near_of, far_of = cross_coefficients(ties, odd, span, i)
        pull = near_of[0] * near_fields[0] + far_of[0] * far_fields[0]
        for j in range(1, span):
            pull = pull + near_of[j] * near_fields[j] + far_of[j] * far_fields[j]
        put(total, i, span, take(image, i, span) - coupling[i : i + 1, :] * pull)
    if with_sums:
        first = (earlier.shape[1] - image.shape[1]) // 2
        last = jnp.sum(earlier[:, pl.ds(first, image.shape[1]), :] * total[...])
        lane = lax.broadcasted_iota(jnp.int32, (1, LANES), 1)
        spread[...] = jnp.broadcast_to(jnp.where(lane == 3, last, sums[...]), spread.shape)
    else:
        clear_outside(index, total, span)
        for k in range(sent.shape[0]):
            sent[k] = total[k, pl.ds(span, sent.shape[1]), :]


def last_kernel(gathered, guess, residual, image, second, step_out, residual_out):
    sums = jnp.sum(gathered[...], axis=0, keepdims=True)
    rr, ra, aa, ab = (sums[:, k : k + 1] for k in range(4))
    alpha = rr / ra
    rr_next = alpha * (alpha * aa - ra)
    beta = rr_next / rr
    product = ra - 2.0 * alpha * aa + alpha * alpha * ab
    alpha_next = rr_next / (product - beta * rr_next / alpha)
    one = alpha + alpha_next * (1.0 + beta)
    two = alpha_next * alpha
    hours, span, width = step_out.shape
    rows = hours * span

    def inner(ref, k):
        return ref[k, pl.ds((ref.shape[1] - rows) // 2, rows), :]

    for k in range(width // LANES):
        lanes = pl.ds(LANES * k, LANES)
        r, a = inner(residual, k), inner(image, k)
        step = guess[k, pl.ds(0, rows), :] + one * r - two * a
        left = r - one * a + two * second[k]
        step_out[:, :, lanes] = step.reshape(hours, span, LANES)
        residual_out[:, :, lanes] = left.reshape(hours, span, LANES)


def swap(value, axis, step, name):
    count = lax.axis_size(axis)
    with jax.named_scope(name):
        return lax.ppermute(value, axis, [(i, i ^ step) for i in range(count)])


def exchange(field, name):
    groups = lax.axis_size("area")
    far_pairs = [(i, i + 1) for i in range(1, groups - 1, 2)]
    with jax.named_scope(name + "_far"):
        far = lax.ppermute(field, "area", far_pairs + [(j, i) for i, j in far_pairs])
    return swap(field, "area", 1, name + "_near"), far


def adjacent_hours(up, down, name):
    ups = [(i, i + 1) for i in range(lax.axis_size("tm") - 1)]
    with jax.named_scope(name + "_before"):
        before = lax.ppermute(up, "tm", ups)
    with jax.named_scope(name + "_after"):
        after = lax.ppermute(down, "tm", [(j, i) for i, j in ups])
    return before, after


def body(
    gradient,
    barrier,
    slack,
    hess_diag,
    tile,
    ramp_weight,
    bus_coupling,
    tie_offset,
    tie_admittance,
    con_sens,
    con_weight,
    con_owner,
    step_guess,
):
    hours, span, width = gradient.shape
    total_areas = tie_offset.shape[0]
    groups, members = lax.axis_size("area"), lax.axis_size("tm")
    chips = groups // 2
    assert members == span and span == TIES and span & (span - 1) == 0
    assert chips & (chips - 1) == 0 and width % LANES == 0
    rows_held = con_sens.shape[0]
    cap = max(2, (2 * rows_held + total_areas - 1) // total_areas)
    slots = groups * cap
    deep = 2
    assert hours + 2 * deep <= HOUR_LANES and rows_held <= width
    blocks = width // LANES
    rows = hours * span
    member, group = lax.axis_index("tm"), lax.axis_index("area")
    index = jnp.stack([group // 2, group % 2, member, jnp.int32(members)]).astype(jnp.int32)

    owner = con_owner.reshape(1, rows_held)
    weight = con_weight.T
    parts = width // WIDE
    chunk = (parts + 1) * cap
    local = (parts * span + 1) * cap
    *away, here, other = call(
        functools.partial(pack_kernel, span, cap, hours),
        [f32_shape(2 * chunk, WIDE)] * (chips - 1)
        + [f32_shape(local, WIDE)] * 2,
        [SCALARS] + [IN_HBM] * 3,
        landing(owner, con_sens, weight),
    )(index, *in_hbm(owner, con_sens, weight))
    arrived = [swap(a, "area", 2 * (k + 1), "rows_chips") for k, a in enumerate(away)]
    beside = swap(other, "area", 1, "rows_beside")
    crossed = swap(jnp.concatenate([a[chunk:] for a in arrived], axis=0), "area", 1, "rows_cores")
    field_shape = f32_shape(blocks, rows, LANES)
    natural = (step_guess, gradient, slack, hess_diag)
    guess, right_side, diagonal_in = call(
        fields_kernel,
        [f32_shape(blocks, rows + 2 * span, LANES), field_shape, field_shape],
        [SCALARS] + [IN_HBM] * 5 + [UNREAD],
        landing(*natural, bus_coupling),
    )(barrier, *in_hbm(*natural, bus_coupling), here)
    near_guess, far_guess = exchange(guess, "guess")

    tile_shape = jax.ShapeDtypeStruct(tile.shape, BF16)
    tables = (tie_offset.T, tie_admittance.T)
    tile_high, tile_low, ties = call(
        halves_kernel,
        [tile_shape, tile_shape, f32_shape(2 * span, span)],
        [SCALARS] + [IN_HBM] * 3 + [UNREAD],
        [pltpu.SMEM(a.shape, a.dtype) for a in tables]
        + [pltpu.VMEM(tile.shape, F32), pltpu.SemaphoreType.DMA((2 + span,))],
        out_specs=[WHOLE, WHOLE, SCALARS],
    )(index, *in_hbm(tile, *tables), right_side)

    weights = call(
        functools.partial(weights_kernel, span, cap),
        f32_shape(span, hours, slots),
        [WHOLE] * (3 + len(arrived)),
    )(here, beside, crossed, *arrived)
    piece = jnp.concatenate(
        [
            a[at : at + parts * cap]
            for k, ref in enumerate(arrived)
            for a, at in ((ref, 0), (crossed, chunk * k))
        ],
        axis=0,
    )
    pieces = [piece] + [swap(piece, "tm", step, "rows_members") for step in range(1, members)]

    edge_rows = (3 * deep - 1) * span + 2 * deep
    partial, diagonal, up, down = call(
        functools.partial(first_kernel, span, deep),
        [field_shape] * 2 + [f32_shape(blocks, edge_rows, LANES)] * 2,
        [SCALARS] * 2 + [WHOLE] * 10,
        flops=FIRST,
    )(
        index,
        ties,
        guess,
        right_side,
        diagonal_in,
        near_guess,
        far_guess,
        weights,
        tile_high,
        tile_low,
        ramp_weight,
        bus_coupling,
    )
    before, after = adjacent_hours(up, down, "partial")

    sens_shape = jax.ShapeDtypeStruct((span, slots, width), BF16)
    deep_shape = f32_shape(blocks, rows + 2 * deep * span, LANES)
    next_shape = f32_shape(blocks, rows + 2 * (deep - 1) * span, LANES)
    residual, residual_sent, sens_high, sens_low, diagonal, owned_weight = call(
        functools.partial(owned_kernel, span, cap, deep),
        [
            deep_shape,
            next_shape,
            sens_shape,
            sens_shape,
            next_shape,
            f32_shape(span, hours + 2 * deep, slots),
        ],
        [SCALARS] + [WHOLE] * (9 + span),
        [pltpu.VMEM(deep_shape.shape, F32)] * 2,
    )(index, guess, partial, diagonal, weights, before, after, ramp_weight, here, beside, *pieces)

    def local_image(field, skip, earlier=None):
        shape = f32_shape(blocks, field.shape[1] - 2 * span, LANES)
        summed = earlier is not None
        return call(
            functools.partial(local_kernel, span, skip, summed),
            (shape, f32_shape(1, LANES)) if summed else shape,
            [SCALARS, SCALARS] + [WHOLE] * (9 + summed),
        )(
            index,
            ties,
            field,
            diagonal,
            ramp_weight,
            bus_coupling,
            tile_high,
            tile_low,
            sens_high,
            sens_low,
            owned_weight,
            *([earlier] if summed else []),
        )

    near, far = exchange(residual_sent, "residual")
    image = local_image(residual, 1)
    image, image_sent = call(
        functools.partial(cross_kernel, span, False),
        (f32_shape(*image.shape), field_shape),
        [SCALARS, SCALARS] + [WHOLE] * 6,
    )(index, ties, image, near, far, near_guess, far_guess, bus_coupling)

    near, far = exchange(image_sent, "image")
    second, sums = local_image(image, 2, residual)
    second, spread = call(
        functools.partial(cross_kernel, span, True),
        (field_shape, f32_shape(groups * members, LANES)),
        [SCALARS, SCALARS] + [WHOLE] * 8,
    )(index, ties, second, near, far, near_guess, far_guess, bus_coupling, image, sums)
    gathered = lax.all_to_all(spread, ("tm", "area"), split_axis=0, concat_axis=0, tiled=True)
    out_shape = f32_shape(hours, span, width)
    return tuple(
        call(
            last_kernel,
            (out_shape, out_shape),
            [WHOLE] * 5,
        )(gathered, guess, residual, image, second)
    )


def solution(mesh):
    field = P("tm", "area", None)
    placed = (
        field,
        P(),
        field,
        field,
        P("area", None, None),
        P("area", None),
        P("area", None),
        P(),
        P(),
        P("area", None),
        P("area", "tm"),
        P("area", None),
        field,
    )
    return jax.shard_map(
        body, mesh=mesh, in_specs=placed, out_specs=(field, field), check_vma=False
    )
```

```python
import functools
import jax
import jax.numpy as jnp
from jax import lax
from jax.experimental import pallas as pl
from jax.experimental.pallas import tpu as pltpu
from jax.sharding import PartitionSpec as P

TIES = 4
HOUR_LANES = 64
LANES = 128
FIRST = 10**10
WIDE = 256
F32 = jnp.float32
BF16 = jnp.bfloat16
VMEM_LIMIT = 12 * 1024 * 1024

WHOLE = pl.BlockSpec(memory_space=pltpu.VMEM)
SCALARS = pl.BlockSpec(memory_space=pltpu.SMEM)
UNREAD = pl.BlockSpec(memory_space=pl.ANY)
IN_HBM = pl.BlockSpec(memory_space=pltpu.HBM)


def call(kernel, out_shape, in_specs, scratch=(), flops=1, out_specs=None):
    many = isinstance(out_shape, (tuple, list))
    if out_specs is None:
        out_specs = [WHOLE] * len(out_shape) if many else WHOLE
    inner = getattr(kernel, "func", kernel)
    return pl.pallas_call(
        kernel,
        name=inner.__name__,
        out_shape=out_shape,
        in_specs=in_specs,
        out_specs=out_specs,
        scratch_shapes=scratch,
        compiler_params=pltpu.CompilerParams(vmem_limit_bytes=VMEM_LIMIT),
        cost_estimate=pl.CostEstimate(flops=flops, bytes_accessed=1, transcendentals=0),
    )


def landing(*operands):
    return [pltpu.VMEM(a.shape, a.dtype) for a in operands] + [
        pltpu.SemaphoreType.DMA((len(operands),))
    ]


def in_hbm(*operands):
    return [pltpu.with_memory_space_constraint(a, pltpu.HBM) for a in operands]


def fetch(sources, targets, semaphores):
    copies = [
        pltpu.make_async_copy(source, target, semaphores.at[k])
        for k, (source, target) in enumerate(zip(sources, targets))
    ]
    for copy in copies:
        copy.start()
    return copies


def f32_shape(*shape):
    return jax.ShapeDtypeStruct(shape, F32)


def two_parts(value):
    high = value.astype(BF16)
    return high, (value - high.astype(F32)).astype(BF16)


def three_parts(value):
    high = value.astype(BF16)
    rest = value - high.astype(F32)
    middle = rest.astype(BF16)
    return high, middle, (rest - middle.astype(F32)).astype(BF16)


def dot(left, right, contract_right=0):
    return lax.dot_general(
        left, right, (((1,), (contract_right,)), ((), ())), preferred_element_type=F32
    )


def split_dot(left, right_high, right_low, contract_right=0):
    high, low = two_parts(left)
    return (
        dot(high, right_high, contract_right)
        + dot(low, right_high, contract_right)
        + dot(high, right_low, contract_right)
    )


def take(ref, area, span, first=0, hours=None):
    hours = ref.shape[1] // span - first if hours is None else hours
    rows = pl.ds(area + span * first, hours, stride=span)
    return jnp.concatenate([ref[k, rows, :] for k in range(ref.shape[0])], axis=1)


def put(ref, area, span, value):
    rows = pl.ds(area, value.shape[0], stride=span)
    for k in range(ref.shape[0]):
        ref[k, rows, :] = value[:, LANES * k : LANES * (k + 1)]


def row_of(ref, row):
    return jnp.concatenate([ref[k, row : row + 1, :] for k in range(ref.shape[0])], axis=1)


def keys_of(owner, cap):
    rows = owner.shape[1]
    owner_row = owner[...].astype(F32)
    owner_column = jnp.transpose(jnp.broadcast_to(owner_row, (LANES, rows)))[:, 0:1]
    earlier = lax.broadcasted_iota(jnp.int32, (rows, rows), 0) < lax.broadcasted_iota(
        jnp.int32, (rows, rows), 1
    )
    same = jnp.where(earlier & (owner_column == owner_row), 1.0, 0.0)
    return owner_row * cap + jnp.sum(same, axis=0, keepdims=True)


def chip_steps(chips, core):
    return [k % (chips - 1) + 1 for k in range(core, chips - 1 + core)]


def member_steps(members, core):
    steps = list(range(members))
    return steps[:1] + steps[2:0:-1] + steps[3:] if core else steps


def by_core(steps_of, count, core):
    return [jnp.where(core == 1, b, a) for a, b in zip(steps_of(count, 0), steps_of(count, 1))]


def selected(position, values):
    total = values[0]
    for k, value in enumerate(values[1:]):
        total = jnp.where(position == k + 1, value, total)
    return total


def marks_of(keys, area, rank, cap):
    return jnp.where((area * cap + rank).astype(F32) == keys, 1.0, 0.0).astype(BF16)


def pack_kernel(span, cap, index, *refs):
    *away, here, beside, guess_out = refs[5:-6]
    owner, sens, weight, guess, coupling, semaphores = refs[-6:]
    copies = fetch(refs[:5], refs[-6:-1], semaphores)
    hours = weight.shape[0]
    chip, core, member = index[0], index[1], index[2]
    blocks = owner.shape[1]
    parts = sens.shape[1] // WIDE
    copies[0].wait()
    keys = keys_of(owner, cap)
    slot = lax.broadcasted_iota(jnp.int32, (2 * cap * (len(away) + 1), blocks), 0)
    chip_step = selected(
        slot // (2 * cap), [jnp.int32(0)] + by_core(chip_steps, len(away) + 1, core)
    )
    group = (chip ^ chip_step) * 2 + (core ^ (slot // cap % 2))
    local = lax.broadcasted_iota(jnp.int32, (2 * span * cap, blocks), 0)
    local_group = chip * 2 + (core ^ (local // (span * cap)))
    other = local // (span * cap) == 1
    member_step = jnp.where(
        other,
        selected(local // cap % span, by_core(member_steps, span, 1 - core)),
        selected(local // cap % span, by_core(member_steps, span, core)),
    )
    local_area = local_group * span + (member ^ member_step)
    sens_marks = jnp.concatenate(
        [
            marks_of(keys, group * span + member, slot % cap, cap)[2 * cap :],
            marks_of(keys, local_area, local % cap, cap),
        ],
        axis=0,
    )
    area_marks = [marks_of(keys, group * span + k, slot % cap, cap) for k in range(span)]
    copies[2].wait()
    gap = jnp.zeros((LANES - hours, blocks), F32)
    by_block = jnp.transpose(jnp.concatenate([weight[...], gap], axis=0))
    left_parts = two_parts(by_block)
    right_parts = two_parts(pltpu.roll(by_block, HOUR_LANES, 1))
    weights = jnp.concatenate(
        [
            sum(
                dot(area_marks[2 * pair], a) + dot(area_marks[2 * pair + 1], b)
                for a, b in zip(left_parts, right_parts)
            )
            for pair in range(span // 2)
        ],
        axis=1,
    )
    copies[1].wait()
    high, low = two_parts(sens[...])
    rows = dot(sens_marks, high) + dot(sens_marks, low)
    for k in range(len(away)):
        for core_step in range(2):
            row, at = cap * (2 * k + core_step), cap * (parts + 1) * core_step
            for part in range(parts):
                lanes = slice(WIDE * part, WIDE * (part + 1))
                away[k][pl.ds(at + cap * part, cap), :] = rows[row : row + cap, lanes]
            away[k][pl.ds(at + cap * parts, cap), :] = weights[2 * cap + row :][:cap]
    count = span * cap
    for core_step, out in ((0, here), (1, beside)):
        row = 2 * cap * len(away) + count * core_step
        for part in range(parts):
            lanes = slice(WIDE * part, WIDE * (part + 1))
            out[pl.ds(count * part, count), :] = rows[row : row + count, lanes]
        out[pl.ds(count * parts, cap), :] = weights[cap * core_step :][:cap]
    for copy in copies[3:]:
        copy.wait()
    hours, span, width = guess.shape
    rows = hours * span
    shape = (rows, LANES)
    for k in range(width // LANES):
        lanes = pl.ds(LANES * k, LANES)
        guess_out[k, pl.ds(0, rows), :] = guess[:, :, lanes].reshape(shape)
        guess_out[k, pl.ds(rows, span), :] = coupling[:, LANES * k : LANES * (k + 1)]
        guess_out[k, pl.ds(rows + span, span), :] = jnp.zeros((span, LANES), F32)


def prepare_kernel(index, barrier, *refs):
    tile_high, tile_low, right_out, diagonal_out, ties = refs[-12:-7]
    gradient, slack, hess, offsets, gains, tile, semaphores = refs[-7:]
    span = tile.shape[0]
    copies = fetch(
        refs[:5] + tuple(refs[5].at[i] for i in range(span)),
        (gradient, slack, hess, offsets, gains) + tuple(tile.at[i] for i in range(span)),
        semaphores,
    )
    for copy in copies[:5]:
        copy.wait()
    hours, span, width = slack.shape
    shape = (hours * span, LANES)
    for k in range(width // LANES):
        lanes = pl.ds(LANES * k, LANES)
        slack_rows = slack[:, :, lanes].reshape(shape)
        right_out[k] = barrier[0] / slack_rows - gradient[:, :, lanes].reshape(shape)
        diagonal_out[k] = hess[:, :, lanes].reshape(shape) + barrier[0] / (
            slack_rows * slack_rows
        )
    first = (index[0] * 2 + index[1] - 1) * span
    for i in range(2 * span):
        area = jnp.maximum(first + i, 0)
        for step in range(span):
            ties[i, step] = 0.0
        for k in range(offsets.shape[0]):
            step = offsets[k, area] - 1
            ties[i, step] = ties[i, step] + gains[k, area]
    for i in range(span):
        copies[5 + i].wait()
        high, low = two_parts(tile[i])
        tile_high[i] = high
        tile_low[i] = low


def weights_kernel(span, cap, deep, here, beside, crossed, *refs):
    *arrived, weights, outer = refs
    hours = weights.shape[1]
    chunk = arrived[0].shape[0] // 2
    pieces = [ref[pl.ds(ref.shape[0] - cap, cap), :] for ref in (here, beside)]
    for k, ref in enumerate(arrived):
        pieces.append(ref[pl.ds(chunk - cap, cap), :])
        pieces.append(crossed[pl.ds(chunk * (k + 1) - cap, cap), :])
    by_slot = jnp.concatenate(pieces, axis=0)
    for pair in range(span // 2):
        turned = jnp.transpose(by_slot[:, LANES * pair : LANES * (pair + 1)])
        for half in range(2):
            weights[2 * pair + half] = turned[HOUR_LANES * half :][:hours]
    for j in range(2 * deep):
        hour = j if j < deep else hours - 2 * deep + j
        for area in range(span):
            outer[
                pl.ds(span // 2 * j + area // 2, 1), pl.ds(LANES * (area % 2), LANES)
            ] = weights[area, pl.ds(hour, 1), :]


def upper(ties, span, i, j):
    return ties[span + i, j + span - i - 1] if j <= i else 0.0


def lower(ties, span, i, j):
    return ties[j, i + span - j - 1] if j >= i else 0.0


def local_tie(ties, span, i, j):
    a, b = min(i, j), max(i, j)
    return ties[span + a, b - a - 1]


def cross_coefficients(ties, odd, span, i):
    near, far = [], []
    for j in range(span):
        up, down = upper(ties, span, i, j), lower(ties, span, i, j)
        near.append(jnp.where(odd, down, up))
        far.append(jnp.where(odd, up, down))
    return near, far


def both_hours(field, area, span, hours):
    return take(field, area, span, 0, hours) + take(field, area, span, 2, hours)


def both_hours_inside(own):
    blank = jnp.zeros((1, own.shape[1]), F32)
    earlier = jnp.concatenate([blank, own[: own.shape[0] - 1]], axis=0)
    return earlier + jnp.concatenate([own[1:], blank], axis=0)


def local_pull(ties, coupling, field, span, i, hours, first=1):
    pull = None
    for j in range(span):
        if j != i:
            term = local_tie(ties, span, i, j) * (
                coupling[j : j + 1, :] * take(field, j, span, first, hours)
            )
            pull = term if pull is None else pull + term
    return pull


def first_kernel(
    span,
    deep,
    index,
    ties,
    guess,
    right,
    diagonal_in,
    near,
    far,
    tile_high,
    tile_low,
    ramp,
    coupling,
    partial,
    diagonal,
    up,
    down,
):
    odd = index[1] == 1
    blocks, rows = right.shape[:2]
    hours = rows // span
    near_coupling = [row_of(near, rows + j) for j in range(span)]
    far_coupling = [row_of(far, rows + j) for j in range(span)]
    near_fields = [near_coupling[j] * take(near, j, span, 0, hours) for j in range(span)]
    far_fields = [far_coupling[j] * take(far, j, span, 0, hours) for j in range(span)]
    for i in range(span):
        own = take(guess, i, span, 0, hours)
        own_coupling = coupling[i : i + 1, :]
        own_ramp = ramp[i : i + 1, :]
        near_of, far_of = cross_coefficients(ties, odd, span, i)
        strength = jnp.zeros_like(own_coupling)
        pull = local_pull(ties, coupling, guess, span, i, hours, 0)
        for j in range(span):
            if j != i:
                strength = strength + local_tie(ties, span, i, j) * coupling[j : j + 1, :]
            strength = strength + near_of[j] * near_coupling[j] + far_of[j] * far_coupling[j]
            pull = pull + near_of[j] * near_fields[j] + far_of[j] * far_fields[j]
        folded = take(diagonal_in, i, span) + (2.0 * own_ramp + own_coupling * strength)
        put(diagonal, i, span, folded)
        image = (
            folded * own
            + split_dot(own, tile_high[i], tile_low[i])
            - own_ramp * both_hours_inside(own)
            - own_coupling * pull
        )
        put(partial, i, span, take(right, i, span) - image)
    for k in range(blocks):
        for out, low in ((up, False), (down, True)):
            at = 0
            for source, count in (
                (partial, deep * span),
                (guess, deep * span),
                (diagonal, (deep - 1) * span),
            ):
                start = 0 if low else rows - count
                out[k, pl.ds(at, count), :] = source[k, pl.ds(start, count), :]
                at += count


def security(own, high, low, weight):
    flows = split_dot(own, high, low, 1)
    return split_dot(flows * weight, high, low)


def clear_outside(index, target, count):
    blocks, rows = target.shape[:2]
    keep_first = jnp.where(index[2] == 0, 0.0, 1.0)
    keep_last = jnp.where(index[2] == index[3] - 1, 0.0, 1.0)
    for k in range(blocks):
        target[k, 0:count, :] = target[k, 0:count, :] * keep_first
        target[k, rows - count : rows, :] = target[k, rows - count : rows, :] * keep_last


def owned_kernel(
    span,
    cap,
    deep,
    index,
    guess_in,
    partial_in,
    diagonal_in,
    weights_in,
    before,
    after,
    ramp,
    here,
    beside,
    *refs,
):
    pieces, outs = refs[:span], refs[span:]
    residual, sent, high_out, low_out, diagonal, weights, guess, partial = outs
    blocks, rows = partial_in.shape[:2]
    for k in range(blocks):
        at = 0
        for target, middle, edge in (
            (partial, partial_in, deep * span),
            (guess, guess_in, deep * span),
            (diagonal, diagonal_in, (deep - 1) * span),
        ):
            target[k, pl.ds(0, edge), :] = before[k, pl.ds(at, edge), :]
            target[k, pl.ds(edge, rows), :] = middle[k, pl.ds(0, rows), :]
            target[k, pl.ds(edge + rows, edge), :] = after[k, pl.ds(at, edge), :]
            at += edge
        edge = ramp[:, LANES * k : LANES * (k + 1)]
        for hour, other in (
            (deep - 1, deep),
            (deep, deep - 1),
            (rows // span + deep - 1, rows // span + deep),
            (rows // span + deep, rows // span + deep - 1),
        ):
            target = pl.ds(span * hour, span)
            partial[k, target, :] = (
                partial[k, target, :] + edge * guess[k, pl.ds(span * other, span), :]
            )
    steps = by_core(member_steps, span, index[1])
    count = pieces[0].shape[0] - span * deep

    def outer_hours(area, other, first):
        total = jnp.zeros((deep, LANES), F32)
        for step in range(1, span):
            value = jnp.concatenate(
                [
                    pieces[step][
                        pl.ds(count + span // 2 * (first + j) + area // 2, 1),
                        pl.ds(LANES * (area % 2), LANES),
                    ]
                    for j in range(deep)
                ],
                axis=0,
            )
            total = jnp.where(index[2] ^ steps[step] == other, value, total)
        return total

    for area in range(span):
        weights[area] = jnp.concatenate(
            [
                outer_hours(area, index[2] - 1, deep),
                weights_in[area],
                outer_hours(area, index[2] + 1, 0),
            ],
            axis=0,
        )
    parts = guess.shape[0] * LANES // WIDE
    group = count // (parts * cap)
    terms = []
    for step in range(span):
        area = index[2] ^ steps[step]
        wide = []
        for part in range(parts):
            at = cap * (span * part + step)
            rows = [here[pl.ds(at, cap), :], beside[pl.ds(at, cap), :]]
            rows += [
                pieces[step][pl.ds(cap * (parts * k + part), cap), :] for k in range(group)
            ]
            wide.append(jnp.concatenate(rows, axis=0))
        high, low = two_parts(jnp.concatenate(wide, axis=1))
        high_out[step] = high
        low_out[step] = low
        term = security(take(guess, area, span), high, low, weights[area])
        terms.append(take(partial, area, span) - term)
    for step in range(span):
        put(residual, index[2] ^ steps[step], span, terms[step])
    clear_outside(index, residual, deep * span)
    for k in range(sent.shape[0]):
        sent[k] = residual[k, pl.ds(span, sent.shape[1]), :]


def local_kernel(
    span,
    skip,
    with_sums,
    index,
    ties,
    field,
    diagonal,
    ramp,
    coupling,
    tile_high,
    tile_low,
    sens_high,
    sens_low,
    weights,
    *refs,
):
    if with_sums:
        earlier, image, sums = refs
    else:
        (image,) = refs
    hours = image.shape[1] // span
    steps = by_core(member_steps, span, index[1])
    for i in range(span):
        value = (
            take(diagonal, i, span, skip - 1, hours) * take(field, i, span, 1, hours)
            + split_dot(take(field, i, span, 1, hours), tile_high[i], tile_low[i])
            - ramp[i : i + 1, :] * both_hours(field, i, span, hours)
            - coupling[i : i + 1, :] * local_pull(ties, coupling, field, span, i, hours)
        )
        put(image, i, span, value)
    terms = []
    for step in range(span):
        area = index[2] ^ steps[step]
        weight = weights[area][skip : skip + hours]
        own = take(field, area, span, 1, hours)
        terms.append(security(own, sens_high[step], sens_low[step], weight))
    for step in range(span):
        area = index[2] ^ steps[step]
        put(image, area, span, take(image, area, span) + terms[step])
    if with_sums:
        count = image.shape[1]
        first = (earlier.shape[1] - count) // 2
        a, b = earlier[:, pl.ds(first, count), :], field[:, pl.ds(span, count), :]
        sums[...] = lanes_of([jnp.sum(a * a), jnp.sum(a * b), jnp.sum(b * b)])


def lanes_of(values):
    lane = lax.broadcasted_iota(jnp.int32, (1, LANES), 1)
    row = jnp.zeros((1, LANES), F32)
    for position, value in enumerate(values):
        row = jnp.where(lane == position, value, row)
    return row


def cross_kernel(
    span, with_sums, index, ties, image, near, far, near_first, far_first, coupling, *refs
):
    if with_sums:
        earlier, sums, total, spread = refs
    else:
        total, sent = refs
    odd = index[1] == 1
    hours = image.shape[1] // span
    count = near_first.shape[1] - 2 * span
    near_fields = [row_of(near_first, count + j) * take(near, j, span) for j in range(span)]
    far_fields = [row_of(far_first, count + j) * take(far, j, span) for j in range(span)]
    for i in range(span):
        near_of, far_of = cross_coefficients(ties, odd, span, i)
        pull = near_of[0] * near_fields[0] + far_of[0] * far_fields[0]
        for j in range(1, span):
            pull = pull + near_of[j] * near_fields[j] + far_of[j] * far_fields[j]
        put(total, i, span, take(image, i, span) - coupling[i : i + 1, :] * pull)
    if with_sums:
        first = (earlier.shape[1] - image.shape[1]) // 2
        last = jnp.sum(earlier[:, pl.ds(first, image.shape[1]), :] * total[...])
        lane = lax.broadcasted_iota(jnp.int32, (1, LANES), 1)
        spread[...] = jnp.broadcast_to(jnp.where(lane == 3, last, sums[...]), spread.shape)
    else:
        clear_outside(index, total, span)
        for k in range(sent.shape[0]):
            sent[k] = total[k, pl.ds(span, sent.shape[1]), :]


def last_kernel(gathered, guess, residual, image, second, step_out, residual_out):
    sums = jnp.sum(gathered[...], axis=0, keepdims=True)
    rr, ra, aa, ab = (sums[:, k : k + 1] for k in range(4))
    alpha = rr / ra
    rr_next = alpha * (alpha * aa - ra)
    beta = rr_next / rr
    product = ra - 2.0 * alpha * aa + alpha * alpha * ab
    alpha_next = rr_next / (product - beta * rr_next / alpha)
    one = alpha + alpha_next * (1.0 + beta)
    two = alpha_next * alpha
    hours, span, width = step_out.shape
    rows = hours * span

    def inner(ref, k):
        return ref[k, pl.ds((ref.shape[1] - rows) // 2, rows), :]

    for k in range(width // LANES):
        lanes = pl.ds(LANES * k, LANES)
        r, a = inner(residual, k), inner(image, k)
        step = guess[k, pl.ds(0, rows), :] + one * r - two * a
        left = r - one * a + two * second[k]
        step_out[:, :, lanes] = step.reshape(hours, span, LANES)
        residual_out[:, :, lanes] = left.reshape(hours, span, LANES)


def swap(value, axis, step, name):
    count = lax.axis_size(axis)
    with jax.named_scope(name):
        return lax.ppermute(value, axis, [(i, i ^ step) for i in range(count)])


def swap_by_core(value, axis, steps_of, position, name):
    members, groups = lax.axis_size("tm"), lax.axis_size("area")
    pairs = []
    for member in range(members):
        for group in range(groups):
            if axis == "tm":
                other = (member ^ steps_of(members, group % 2)[position]) * groups + group
            else:
                step = steps_of(groups // 2, group % 2)[position]
                other = member * groups + (group ^ (2 * step))
            pairs.append((member * groups + group, other))
    with jax.named_scope(name):
        return lax.ppermute(value, ("tm", "area"), pairs)


def exchange(field, name):
    groups = lax.axis_size("area")
    far_pairs = [(i, i + 1) for i in range(1, groups - 1, 2)]
    with jax.named_scope(name + "_far"):
        far = lax.ppermute(field, "area", far_pairs + [(j, i) for i, j in far_pairs])
    return swap(field, "area", 1, name + "_near"), far


def adjacent_hours(up, down, name):
    ups = [(i, i + 1) for i in range(lax.axis_size("tm") - 1)]
    with jax.named_scope(name + "_before"):
        before = lax.ppermute(up, "tm", ups)
    with jax.named_scope(name + "_after"):
        after = lax.ppermute(down, "tm", [(j, i) for i, j in ups])
    return before, after


def body(
    gradient,
    barrier,
    slack,
    hess_diag,
    tile,
    ramp_weight,
    bus_coupling,
    tie_offset,
    tie_admittance,
    con_sens,
    con_weight,
    con_owner,
    step_guess,
):
    hours, span, width = gradient.shape
    total_areas = tie_offset.shape[0]
    groups, members = lax.axis_size("area"), lax.axis_size("tm")
    chips = groups // 2
    assert members == span and span == TIES and span & (span - 1) == 0
    assert chips & (chips - 1) == 0 and width % LANES == 0
    rows_held = con_sens.shape[0]
    cap = max(2, (2 * rows_held + total_areas - 1) // total_areas)
    slots = groups * cap
    deep = 2
    assert hours + 2 * deep <= HOUR_LANES and rows_held <= width
    blocks = width // LANES
    rows = hours * span
    member, group = lax.axis_index("tm"), lax.axis_index("area")
    index = jnp.stack([group // 2, group % 2, member, jnp.int32(members)]).astype(jnp.int32)

    owner = con_owner.reshape(1, rows_held)
    weight = con_weight.T
    parts = width // WIDE
    chunk = (parts + 1) * cap
    local = (parts * span + 1) * cap
    field_shape = f32_shape(blocks, rows, LANES)
    sources = (owner, con_sens, weight, step_guess, bus_coupling)
    *away, here, other, guess = call(
        functools.partial(pack_kernel, span, cap),
        [f32_shape(2 * chunk, WIDE)] * (chips - 1)
        + [f32_shape(local, WIDE)] * 2
        + [f32_shape(blocks, rows + 2 * span, LANES)],
        [SCALARS] + [IN_HBM] * 5,
        landing(*sources),
    )(index, *in_hbm(*sources))
    arrived = [
        swap_by_core(a, "area", chip_steps, k, "rows_chips") for k, a in enumerate(away)
    ]
    beside = swap(other, "area", 1, "rows_beside")
    crossed = swap(jnp.concatenate([a[chunk:] for a in arrived], axis=0), "area", 1, "rows_cores")
    tile_shape = jax.ShapeDtypeStruct(tile.shape, BF16)
    natural = (gradient, slack, hess_diag)
    tables = (tie_offset.T, tie_admittance.T)
    tile_high, tile_low, right_side, diagonal_in, ties = call(
        prepare_kernel,
        [tile_shape, tile_shape, field_shape, field_shape, f32_shape(2 * span, span)],
        [SCALARS] * 2 + [IN_HBM] * 6 + [UNREAD],
        [pltpu.VMEM(a.shape, F32) for a in natural]
        + [pltpu.SMEM(a.shape, a.dtype) for a in tables]
        + [pltpu.VMEM(tile.shape, F32), pltpu.SemaphoreType.DMA((5 + span,))],
        out_specs=[WHOLE] * 4 + [SCALARS],
    )(index, barrier, *in_hbm(*natural, *tables, tile), here)
    near_guess, far_guess = exchange(guess, "guess")

    weights, outer = call(
        functools.partial(weights_kernel, span, cap, deep),
        [f32_shape(span, hours, slots), f32_shape(span * deep, WIDE)],
        [WHOLE] * (3 + len(arrived)),
    )(here, beside, crossed, *arrived)
    piece = jnp.concatenate(
        [
            a[at : at + parts * cap]
            for k, ref in enumerate(arrived)
            for a, at in ((ref, 0), (crossed, chunk * k))
        ]
        + [outer],
        axis=0,
    )
    pieces = [piece] + [
        swap_by_core(piece, "tm", member_steps, k, "rows_members") for k in range(1, members)
    ]

    edge_rows = (3 * deep - 1) * span
    partial, diagonal, up, down = call(
        functools.partial(first_kernel, span, deep),
        [field_shape] * 2 + [f32_shape(blocks, edge_rows, LANES)] * 2,
        [SCALARS] * 2 + [WHOLE] * 9,
        flops=FIRST,
    )(
        index,
        ties,
        guess,
        right_side,
        diagonal_in,
        near_guess,
        far_guess,
        tile_high,
        tile_low,
        ramp_weight,
        bus_coupling,
    )
    before, after = adjacent_hours(up, down, "partial")

    sens_shape = jax.ShapeDtypeStruct((span, slots, width), BF16)
    deep_shape = f32_shape(blocks, rows + 2 * deep * span, LANES)
    next_shape = f32_shape(blocks, rows + 2 * (deep - 1) * span, LANES)
    residual, residual_sent, sens_high, sens_low, diagonal, owned_weight = call(
        functools.partial(owned_kernel, span, cap, deep),
        [
            deep_shape,
            next_shape,
            sens_shape,
            sens_shape,
            next_shape,
            f32_shape(span, hours + 2 * deep, slots),
        ],
        [SCALARS] + [WHOLE] * (9 + span),
        [pltpu.VMEM(deep_shape.shape, F32)] * 2,
    )(index, guess, partial, diagonal, weights, before, after, ramp_weight, here, beside, *pieces)

    def local_image(field, skip, earlier=None):
        shape = f32_shape(blocks, field.shape[1] - 2 * span, LANES)
        summed = earlier is not None
        return call(
            functools.partial(local_kernel, span, skip, summed),
            (shape, f32_shape(1, LANES)) if summed else shape,
            [SCALARS, SCALARS] + [WHOLE] * (9 + summed),
        )(
            index,
            ties,
            field,
            diagonal,
            ramp_weight,
            bus_coupling,
            tile_high,
            tile_low,
            sens_high,
            sens_low,
            owned_weight,
            *([earlier] if summed else []),
        )

    near, far = exchange(residual_sent, "residual")
    image = local_image(residual, 1)
    image, image_sent = call(
        functools.partial(cross_kernel, span, False),
        (f32_shape(*image.shape), field_shape),
        [SCALARS, SCALARS] + [WHOLE] * 6,
    )(index, ties, image, near, far, near_guess, far_guess, bus_coupling)

    near, far = exchange(image_sent, "image")
    second, sums = local_image(image, 2, residual)
    second, spread = call(
        functools.partial(cross_kernel, span, True),
        (field_shape, f32_shape(groups * members, LANES)),
        [SCALARS, SCALARS] + [WHOLE] * 8,
    )(index, ties, second, near, far, near_guess, far_guess, bus_coupling, image, sums)
    gathered = lax.all_to_all(spread, ("tm", "area"), split_axis=0, concat_axis=0, tiled=True)
    out_shape = f32_shape(hours, span, width)
    return tuple(
        call(
            last_kernel,
            (out_shape, out_shape),
            [WHOLE] * 5,
        )(gathered, guess, residual, image, second)
    )


def solution(mesh):
    field = P("tm", "area", None)
    placed = (
        field,
        P(),
        field,
        field,
        P("area", None, None),
        P("area", None),
        P("area", None),
        P(),
        P(),
        P("area", None),
        P("area", "tm"),
        P("area", None),
        field,
    )
    return jax.shard_map(
        body, mesh=mesh, in_specs=placed, out_specs=(field, field), check_vma=False
    )
```

```python
import functools
import jax
import jax.numpy as jnp
from jax import lax
from jax.experimental import pallas as pl
from jax.experimental.pallas import tpu as pltpu
from jax.sharding import PartitionSpec as P

TIES = 4
HOUR_LANES = 64
LANES = 128
FIRST = 10**10
WIDE = 256
F32 = jnp.float32
BF16 = jnp.bfloat16
VMEM_LIMIT = 12 * 1024 * 1024

WHOLE = pl.BlockSpec(memory_space=pltpu.VMEM)
SCALARS = pl.BlockSpec(memory_space=pltpu.SMEM)
UNREAD = pl.BlockSpec(memory_space=pl.ANY)
IN_HBM = pl.BlockSpec(memory_space=pltpu.HBM)


def call(kernel, out_shape, in_specs, scratch=(), flops=1, out_specs=None):
    many = isinstance(out_shape, (tuple, list))
    if out_specs is None:
        out_specs = [WHOLE] * len(out_shape) if many else WHOLE
    inner = getattr(kernel, "func", kernel)
    return pl.pallas_call(
        kernel,
        name=inner.__name__,
        out_shape=out_shape,
        in_specs=in_specs,
        out_specs=out_specs,
        scratch_shapes=scratch,
        compiler_params=pltpu.CompilerParams(vmem_limit_bytes=VMEM_LIMIT),
        cost_estimate=pl.CostEstimate(flops=flops, bytes_accessed=1, transcendentals=0),
    )


def landing(*operands):
    return [pltpu.VMEM(a.shape, a.dtype) for a in operands] + [
        pltpu.SemaphoreType.DMA((len(operands),))
    ]


def in_hbm(*operands):
    return [pltpu.with_memory_space_constraint(a, pltpu.HBM) for a in operands]


def fetch(sources, targets, semaphores):
    copies = [
        pltpu.make_async_copy(source, target, semaphores.at[k])
        for k, (source, target) in enumerate(zip(sources, targets))
    ]
    for copy in copies:
        copy.start()
    return copies


def f32_shape(*shape):
    return jax.ShapeDtypeStruct(shape, F32)


def two_parts(value):
    high = value.astype(BF16)
    return high, (value - high.astype(F32)).astype(BF16)


def three_parts(value):
    high = value.astype(BF16)
    rest = value - high.astype(F32)
    middle = rest.astype(BF16)
    return high, middle, (rest - middle.astype(F32)).astype(BF16)


def dot(left, right, contract_right=0):
    return lax.dot_general(
        left, right, (((1,), (contract_right,)), ((), ())), preferred_element_type=F32
    )


def split_dot(left, right_high, right_low, contract_right=0):
    high, low = two_parts(left)
    return (
        dot(high, right_high, contract_right)
        + dot(low, right_high, contract_right)
        + dot(high, right_low, contract_right)
    )


def take(ref, area, span, first=0, hours=None):
    hours = ref.shape[1] // span - first if hours is None else hours
    rows = pl.ds(area + span * first, hours, stride=span)
    return jnp.concatenate([ref[k, rows, :] for k in range(ref.shape[0])], axis=1)


def put(ref, area, span, value):
    rows = pl.ds(area, value.shape[0], stride=span)
    for k in range(ref.shape[0]):
        ref[k, rows, :] = value[:, LANES * k : LANES * (k + 1)]


def row_of(ref, row):
    return jnp.concatenate([ref[k, row : row + 1, :] for k in range(ref.shape[0])], axis=1)


def keys_of(owner, cap):
    rows = owner.shape[1]
    owner_row = owner[...].astype(F32)
    owner_column = jnp.transpose(jnp.broadcast_to(owner_row, (LANES, rows)))[:, 0:1]
    earlier = lax.broadcasted_iota(jnp.int32, (rows, rows), 0) < lax.broadcasted_iota(
        jnp.int32, (rows, rows), 1
    )
    same = jnp.where(earlier & (owner_column == owner_row), 1.0, 0.0)
    return owner_row * cap + jnp.sum(same, axis=0, keepdims=True)


def chip_steps(chips, core):
    return [k % (chips - 1) + 1 for k in range(core, chips - 1 + core)]


def member_steps(members, core):
    steps = list(range(members))
    return steps[:1] + steps[2:0:-1] + steps[3:] if core else steps


def by_core(steps_of, count, core):
    return [jnp.where(core == 1, b, a) for a, b in zip(steps_of(count, 0), steps_of(count, 1))]


def selected(position, values):
    total = values[0]
    for k, value in enumerate(values[1:]):
        total = jnp.where(position == k + 1, value, total)
    return total


def marks_of(keys, area, rank, cap):
    return jnp.where((area * cap + rank).astype(F32) == keys, 1.0, 0.0).astype(BF16)


def pack_kernel(span, cap, index, *refs):
    *away, here, beside, guess_out = refs[5:-6]
    owner, sens, weight, guess, coupling, semaphores = refs[-6:]
    copies = fetch(refs[:5], refs[-6:-1], semaphores)
    hours = weight.shape[0]
    chip, core, member = index[0], index[1], index[2]
    blocks = owner.shape[1]
    parts = sens.shape[1] // WIDE
    copies[0].wait()
    keys = keys_of(owner, cap)
    slot = lax.broadcasted_iota(jnp.int32, (2 * cap * (len(away) + 1), blocks), 0)
    chip_step = selected(
        slot // (2 * cap), [jnp.int32(0)] + by_core(chip_steps, len(away) + 1, core)
    )
    group = (chip ^ chip_step) * 2 + (core ^ (slot // cap % 2))
    local = lax.broadcasted_iota(jnp.int32, (2 * span * cap, blocks), 0)
    local_group = chip * 2 + (core ^ (local // (span * cap)))
    other = local // (span * cap) == 1
    member_step = jnp.where(
        other,
        selected(local // cap % span, by_core(member_steps, span, 1 - core)),
        selected(local // cap % span, by_core(member_steps, span, core)),
    )
    local_area = local_group * span + (member ^ member_step)
    sens_marks = jnp.concatenate(
        [
            marks_of(keys, group * span + member, slot % cap, cap)[2 * cap :],
            marks_of(keys, local_area, local % cap, cap),
        ],
        axis=0,
    )
    area_marks = [marks_of(keys, group * span + k, slot % cap, cap) for k in range(span)]
    copies[2].wait()
    gap = jnp.zeros((LANES - hours, blocks), F32)
    by_block = jnp.transpose(jnp.concatenate([weight[...], gap], axis=0))
    left_parts = two_parts(by_block)
    right_parts = two_parts(pltpu.roll(by_block, HOUR_LANES, 1))
    weights = jnp.concatenate(
        [
            sum(
                dot(area_marks[2 * pair], a) + dot(area_marks[2 * pair + 1], b)
                for a, b in zip(left_parts, right_parts)
            )
            for pair in range(span // 2)
        ],
        axis=1,
    )
    copies[1].wait()
    high, low = two_parts(sens[...])
    rows = dot(sens_marks, high) + dot(sens_marks, low)
    for k in range(len(away)):
        for core_step in range(2):
            row, at = cap * (2 * k + core_step), cap * (parts + 1) * core_step
            for part in range(parts):
                lanes = slice(WIDE * part, WIDE * (part + 1))
                away[k][pl.ds(at + cap * part, cap), :] = rows[row : row + cap, lanes]
            away[k][pl.ds(at + cap * parts, cap), :] = weights[2 * cap + row :][:cap]
    count = span * cap
    for core_step, out in ((0, here), (1, beside)):
        row = 2 * cap * len(away) + count * core_step
        for part in range(parts):
            lanes = slice(WIDE * part, WIDE * (part + 1))
            out[pl.ds(count * part, count), :] = rows[row : row + count, lanes]
        out[pl.ds(count * parts, cap), :] = weights[cap * core_step :][:cap]
    for copy in copies[3:]:
        copy.wait()
    hours, span, width = guess.shape
    rows = hours * span
    shape = (rows, LANES)
    for k in range(width // LANES):
        lanes = pl.ds(LANES * k, LANES)
        guess_out[k, pl.ds(0, rows), :] = guess[:, :, lanes].reshape(shape)
        guess_out[k, pl.ds(rows, span), :] = coupling[:, LANES * k : LANES * (k + 1)]
        guess_out[k, pl.ds(rows + span, span), :] = jnp.zeros((span, LANES), F32)


def prepare_kernel(index, barrier, *refs):
    tile_high, tile_low, right_out, diagonal_out, ties = refs[-12:-7]
    gradient, slack, hess, offsets, gains, tile, semaphores = refs[-7:]
    span = tile.shape[0]
    copies = fetch(
        refs[:5] + tuple(refs[5].at[i] for i in range(span)),
        (gradient, slack, hess, offsets, gains) + tuple(tile.at[i] for i in range(span)),
        semaphores,
    )
    for copy in copies[:5]:
        copy.wait()
    hours, span, width = slack.shape
    shape = (hours * span, LANES)
    for k in range(width // LANES):
        lanes = pl.ds(LANES * k, LANES)
        slack_rows = slack[:, :, lanes].reshape(shape)
        right_out[k] = barrier[...] / slack_rows - gradient[:, :, lanes].reshape(shape)
        diagonal_out[k] = hess[:, :, lanes].reshape(shape) + barrier[...] / (
            slack_rows * slack_rows
        )
    first = (index[0] * 2 + index[1] - 1) * span
    for i in range(2 * span):
        area = jnp.maximum(first + i, 0)
        for step in range(span):
            ties[i, step] = 0.0
        for k in range(offsets.shape[0]):
            step = offsets[k, area] - 1
            ties[i, step] = ties[i, step] + gains[k, area]
    for i in range(span):
        copies[5 + i].wait()
        high, low = two_parts(tile[i])
        tile_high[i] = high
        tile_low[i] = low


def weights_kernel(span, cap, deep, here, beside, crossed, *refs):
    *arrived, weights, outer = refs
    hours = weights.shape[1]
    chunk = arrived[0].shape[0] // 2
    pieces = [ref[pl.ds(ref.shape[0] - cap, cap), :] for ref in (here, beside)]
    for k, ref in enumerate(arrived):
        pieces.append(ref[pl.ds(chunk - cap, cap), :])
        pieces.append(crossed[pl.ds(chunk * (k + 1) - cap, cap), :])
    by_slot = jnp.concatenate(pieces, axis=0)
    for pair in range(span // 2):
        turned = jnp.transpose(by_slot[:, LANES * pair : LANES * (pair + 1)])
        for half in range(2):
            weights[2 * pair + half] = turned[HOUR_LANES * half :][:hours]
    for j in range(2 * deep):
        hour = j if j < deep else hours - 2 * deep + j
        for area in range(span):
            outer[
                pl.ds(span // 2 * j + area // 2, 1), pl.ds(LANES * (area % 2), LANES)
            ] = weights[area, pl.ds(hour, 1), :]


def upper(ties, span, i, j):
    return ties[span + i, j + span - i - 1] if j <= i else 0.0


def lower(ties, span, i, j):
    return ties[j, i + span - j - 1] if j >= i else 0.0


def local_tie(ties, span, i, j):
    a, b = min(i, j), max(i, j)
    return ties[span + a, b - a - 1]


def cross_coefficients(ties, odd, span, i):
    near, far = [], []
    for j in range(span):
        up, down = upper(ties, span, i, j), lower(ties, span, i, j)
        near.append(jnp.where(odd, down, up))
        far.append(jnp.where(odd, up, down))
    return near, far


def both_hours(field, area, span, hours):
    return take(field, area, span, 0, hours) + take(field, area, span, 2, hours)


def both_hours_inside(own):
    blank = jnp.zeros((1, own.shape[1]), F32)
    earlier = jnp.concatenate([blank, own[: own.shape[0] - 1]], axis=0)
    return earlier + jnp.concatenate([own[1:], blank], axis=0)


def local_pull(ties, coupling, field, span, i, hours, first=1):
    pull = None
    for j in range(span):
        if j != i:
            term = local_tie(ties, span, i, j) * (
                coupling[j : j + 1, :] * take(field, j, span, first, hours)
            )
            pull = term if pull is None else pull + term
    return pull


def first_kernel(
    span,
    deep,
    index,
    ties,
    guess,
    right,
    diagonal_in,
    near,
    far,
    tile_high,
    tile_low,
    ramp,
    coupling,
    partial,
    diagonal,
    up,
    down,
):
    odd = index[1] == 1
    blocks, rows = right.shape[:2]
    hours = rows // span
    near_coupling = [row_of(near, rows + j) for j in range(span)]
    far_coupling = [row_of(far, rows + j) for j in range(span)]
    near_fields = [near_coupling[j] * take(near, j, span, 0, hours) for j in range(span)]
    far_fields = [far_coupling[j] * take(far, j, span, 0, hours) for j in range(span)]
    for i in range(span):
        own = take(guess, i, span, 0, hours)
        own_coupling = coupling[i : i + 1, :]
        own_ramp = ramp[i : i + 1, :]
        near_of, far_of = cross_coefficients(ties, odd, span, i)
        strength = jnp.zeros_like(own_coupling)
        pull = local_pull(ties, coupling, guess, span, i, hours, 0)
        for j in range(span):
            if j != i:
                strength = strength + local_tie(ties, span, i, j) * coupling[j : j + 1, :]
            strength = strength + near_of[j] * near_coupling[j] + far_of[j] * far_coupling[j]
            pull = pull + near_of[j] * near_fields[j] + far_of[j] * far_fields[j]
        folded = take(diagonal_in, i, span) + (2.0 * own_ramp + own_coupling * strength)
        put(diagonal, i, span, folded)
        image = (
            folded * own
            + split_dot(own, tile_high[i], tile_low[i])
            - own_ramp * both_hours_inside(own)
            - own_coupling * pull
        )
        put(partial, i, span, take(right, i, span) - image)
    for k in range(blocks):
        for out, low in ((up, False), (down, True)):
            at = 0
            for source, count in (
                (partial, deep * span),
                (guess, deep * span),
                (diagonal, (deep - 1) * span),
            ):
                start = 0 if low else rows - count
                out[k, pl.ds(at, count), :] = source[k, pl.ds(start, count), :]
                at += count


def security(own, high, low, weight):
    flows = split_dot(own, high, low, 1)
    return split_dot(flows * weight, high, low)


def clear_outside(index, target, count):
    blocks, rows = target.shape[:2]
    keep_first = jnp.where(index[2] == 0, 0.0, 1.0)
    keep_last = jnp.where(index[2] == index[3] - 1, 0.0, 1.0)
    for k in range(blocks):
        target[k, 0:count, :] = target[k, 0:count, :] * keep_first
        target[k, rows - count : rows, :] = target[k, rows - count : rows, :] * keep_last


def owned_kernel(
    span,
    cap,
    deep,
    index,
    guess_in,
    partial_in,
    diagonal_in,
    weights_in,
    before,
    after,
    ramp,
    here,
    beside,
    *refs,
):
    pieces, outs = refs[:span], refs[span:]
    residual, sent, high_out, low_out, diagonal, weights, guess, partial = outs
    blocks, rows = partial_in.shape[:2]
    for k in range(blocks):
        at = 0
        for target, middle, edge in (
            (partial, partial_in, deep * span),
            (guess, guess_in, deep * span),
            (diagonal, diagonal_in, (deep - 1) * span),
        ):
            target[k, pl.ds(0, edge), :] = before[k, pl.ds(at, edge), :]
            target[k, pl.ds(edge, rows), :] = middle[k, pl.ds(0, rows), :]
            target[k, pl.ds(edge + rows, edge), :] = after[k, pl.ds(at, edge), :]
            at += edge
        edge = ramp[:, LANES * k : LANES * (k + 1)]
        for hour, other in (
            (deep - 1, deep),
            (deep, deep - 1),
            (rows // span + deep - 1, rows // span + deep),
            (rows // span + deep, rows // span + deep - 1),
        ):
            target = pl.ds(span * hour, span)
            partial[k, target, :] = (
                partial[k, target, :] + edge * guess[k, pl.ds(span * other, span), :]
            )
    steps = by_core(member_steps, span, index[1])
    count = pieces[0].shape[0] - span * deep

    def outer_hours(area, other, first):
        total = jnp.zeros((deep, LANES), F32)
        for step in range(1, span):
            value = jnp.concatenate(
                [
                    pieces[step][
                        pl.ds(count + span // 2 * (first + j) + area // 2, 1),
                        pl.ds(LANES * (area % 2), LANES),
                    ]
                    for j in range(deep)
                ],
                axis=0,
            )
            total = jnp.where(index[2] ^ steps[step] == other, value, total)
        return total

    for area in range(span):
        weights[area] = jnp.concatenate(
            [
                outer_hours(area, index[2] - 1, deep),
                weights_in[area],
                outer_hours(area, index[2] + 1, 0),
            ],
            axis=0,
        )
    parts = guess.shape[0] * LANES // WIDE
    group = count // (parts * cap)
    terms = []
    for step in range(span):
        area = index[2] ^ steps[step]
        wide = []
        for part in range(parts):
            at = cap * (span * part + step)
            rows = [here[pl.ds(at, cap), :], beside[pl.ds(at, cap), :]]
            rows += [
                pieces[step][pl.ds(cap * (parts * k + part), cap), :] for k in range(group)
            ]
            wide.append(jnp.concatenate(rows, axis=0))
        high, low = two_parts(jnp.concatenate(wide, axis=1))
        high_out[step] = high
        low_out[step] = low
        term = security(take(guess, area, span), high, low, weights[area])
        terms.append(take(partial, area, span) - term)
    for step in range(span):
        put(residual, index[2] ^ steps[step], span, terms[step])
    clear_outside(index, residual, deep * span)
    for k in range(sent.shape[0]):
        sent[k] = residual[k, pl.ds(span, sent.shape[1]), :]


def local_kernel(
    span,
    skip,
    with_sums,
    index,
    ties,
    field,
    diagonal,
    ramp,
    coupling,
    tile_high,
    tile_low,
    sens_high,
    sens_low,
    weights,
    *refs,
):
    if with_sums:
        earlier, image, sums = refs
    else:
        (image,) = refs
    hours = image.shape[1] // span
    steps = by_core(member_steps, span, index[1])
    for i in range(span):
        value = (
            take(diagonal, i, span, skip - 1, hours) * take(field, i, span, 1, hours)
            + split_dot(take(field, i, span, 1, hours), tile_high[i], tile_low[i])
            - ramp[i : i + 1, :] * both_hours(field, i, span, hours)
            - coupling[i : i + 1, :] * local_pull(ties, coupling, field, span, i, hours)
        )
        put(image, i, span, value)
    terms = []
    for step in range(span):
        area = index[2] ^ steps[step]
        weight = weights[area][skip : skip + hours]
        own = take(field, area, span, 1, hours)
        terms.append(security(own, sens_high[step], sens_low[step], weight))
    for step in range(span):
        area = index[2] ^ steps[step]
        put(image, area, span, take(image, area, span) + terms[step])
    if with_sums:
        count = image.shape[1]
        first = (earlier.shape[1] - count) // 2
        a, b = earlier[:, pl.ds(first, count), :], field[:, pl.ds(span, count), :]
        sums[...] = lanes_of([jnp.sum(a * a), jnp.sum(a * b), jnp.sum(b * b)])


def lanes_of(values):
    lane = lax.broadcasted_iota(jnp.int32, (1, LANES), 1)
    row = jnp.zeros((1, LANES), F32)
    for position, value in enumerate(values):
        row = jnp.where(lane == position, value, row)
    return row


def cross_kernel(
    span, with_sums, index, ties, image, near, far, near_first, far_first, coupling, *refs
):
    if with_sums:
        earlier, sums, total, spread = refs
    else:
        total, sent = refs
    odd = index[1] == 1
    hours = image.shape[1] // span
    count = near_first.shape[1] - 2 * span
    near_fields = [row_of(near_first, count + j) * take(near, j, span) for j in range(span)]
    far_fields = [row_of(far_first, count + j) * take(far, j, span) for j in range(span)]
    for i in range(span):
        near_of, far_of = cross_coefficients(ties, odd, span, i)
        pull = near_of[0] * near_fields[0] + far_of[0] * far_fields[0]
        for j in range(1, span):
            pull = pull + near_of[j] * near_fields[j] + far_of[j] * far_fields[j]
        put(total, i, span, take(image, i, span) - coupling[i : i + 1, :] * pull)
    if with_sums:
        first = (earlier.shape[1] - image.shape[1]) // 2
        last = jnp.sum(earlier[:, pl.ds(first, image.shape[1]), :] * total[...])
        lane = lax.broadcasted_iota(jnp.int32, (1, LANES), 1)
        spread[...] = jnp.broadcast_to(jnp.where(lane == 3, last, sums[...]), spread.shape)
    else:
        clear_outside(index, total, span)
        for k in range(sent.shape[0]):
            sent[k] = total[k, pl.ds(span, sent.shape[1]), :]


def last_kernel(gathered, guess, residual, image, second, step_far, residual_far, *scratch):
    step_out, residual_out, semaphores = scratch
    copies = []
    sums = jnp.sum(gathered[...], axis=0, keepdims=True)
    rr, ra, aa, ab = (sums[:, k : k + 1] for k in range(4))
    alpha = rr / ra
    rr_next = alpha * (alpha * aa - ra)
    beta = rr_next / rr
    product = ra - 2.0 * alpha * aa + alpha * alpha * ab
    alpha_next = rr_next / (product - beta * rr_next / alpha)
    one = alpha + alpha_next * (1.0 + beta)
    two = alpha_next * alpha
    hours, span, width = step_far.shape
    rows = hours * span

    def inner(ref, k):
        return ref[k, pl.ds((ref.shape[1] - rows) // 2, rows), :]

    for k in range(width // LANES):
        lanes = pl.ds(LANES * k, LANES)
        r, a = inner(residual, k), inner(image, k)
        step = guess[k, pl.ds(0, rows), :] + one * r - two * a
        left = r - one * a + two * second[k]
        step_out[k] = step.reshape(hours, span, LANES)
        residual_out[k] = left.reshape(hours, span, LANES)
        for source, target in ((step_out, step_far), (residual_out, residual_far)):
            copies.append(
                pltpu.make_async_copy(
                    source.at[k], target.at[:, :, lanes], semaphores.at[len(copies)]
                )
            )
            copies[-1].start()
    for copy in copies:
        copy.wait()


def swap(value, axis, step, name):
    count = lax.axis_size(axis)
    with jax.named_scope(name):
        return lax.ppermute(value, axis, [(i, i ^ step) for i in range(count)])


def swap_by_core(value, axis, steps_of, position, name):
    members, groups = lax.axis_size("tm"), lax.axis_size("area")
    pairs = []
    for member in range(members):
        for group in range(groups):
            if axis == "tm":
                other = (member ^ steps_of(members, group % 2)[position]) * groups + group
            else:
                step = steps_of(groups // 2, group % 2)[position]
                other = member * groups + (group ^ (2 * step))
            pairs.append((member * groups + group, other))
    with jax.named_scope(name):
        return lax.ppermute(value, ("tm", "area"), pairs)


def exchange(field, name):
    groups = lax.axis_size("area")
    far_pairs = [(i, i + 1) for i in range(1, groups - 1, 2)]
    with jax.named_scope(name + "_far"):
        far = lax.ppermute(field, "area", far_pairs + [(j, i) for i, j in far_pairs])
    return swap(field, "area", 1, name + "_near"), far


def adjacent_hours(up, down, name):
    ups = [(i, i + 1) for i in range(lax.axis_size("tm") - 1)]
    with jax.named_scope(name + "_before"):
        before = lax.ppermute(up, "tm", ups)
    with jax.named_scope(name + "_after"):
        after = lax.ppermute(down, "tm", [(j, i) for i, j in ups])
    return before, after


def body(
    gradient,
    barrier,
    slack,
    hess_diag,
    tile,
    ramp_weight,
    bus_coupling,
    tie_offset,
    tie_admittance,
    con_sens,
    con_weight,
    con_owner,
    step_guess,
):
    hours, span, width = gradient.shape
    total_areas = tie_offset.shape[0]
    groups, members = lax.axis_size("area"), lax.axis_size("tm")
    chips = groups // 2
    assert members == span and span == TIES and span & (span - 1) == 0
    assert chips & (chips - 1) == 0 and width % LANES == 0
    rows_held = con_sens.shape[0]
    cap = max(2, (2 * rows_held + total_areas - 1) // total_areas)
    slots = groups * cap
    deep = 2
    assert hours + 2 * deep <= HOUR_LANES and rows_held <= width
    blocks = width // LANES
    rows = hours * span
    member, group = lax.axis_index("tm"), lax.axis_index("area")
    index = jnp.stack([group // 2, group % 2, member, jnp.int32(members)]).astype(jnp.int32)

    owner = con_owner.reshape(1, rows_held)
    weight = con_weight.T
    parts = width // WIDE
    chunk = (parts + 1) * cap
    local = (parts * span + 1) * cap
    field_shape = f32_shape(blocks, rows, LANES)
    sources = (owner, con_sens, weight, step_guess, bus_coupling)
    *away, here, other, guess = call(
        functools.partial(pack_kernel, span, cap),
        [f32_shape(2 * chunk, WIDE)] * (chips - 1)
        + [f32_shape(local, WIDE)] * 2
        + [f32_shape(blocks, rows + 2 * span, LANES)],
        [SCALARS] + [IN_HBM] * 5,
        landing(*sources),
    )(index, *in_hbm(*sources))
    arrived = [
        swap_by_core(a, "area", chip_steps, k, "rows_chips") for k, a in enumerate(away)
    ]
    beside = swap(other, "area", 1, "rows_beside")
    crossed = swap(jnp.concatenate([a[chunk:] for a in arrived], axis=0), "area", 1, "rows_cores")
    tile_shape = jax.ShapeDtypeStruct(tile.shape, BF16)
    natural = (gradient, slack, hess_diag)
    tables = (tie_offset.T, tie_admittance.T)
    tile_high, tile_low, right_side, diagonal_in, ties = call(
        prepare_kernel,
        [tile_shape, tile_shape, field_shape, field_shape, f32_shape(2 * span, span)],
        [SCALARS, WHOLE] + [IN_HBM] * 6 + [UNREAD],
        [pltpu.VMEM(a.shape, F32) for a in natural]
        + [pltpu.SMEM(a.shape, a.dtype) for a in tables]
        + [pltpu.VMEM(tile.shape, F32), pltpu.SemaphoreType.DMA((5 + span,))],
        out_specs=[WHOLE] * 4 + [SCALARS],
    )(index, barrier.reshape(1, 1), *in_hbm(*natural, *tables, tile), here)
    near_guess, far_guess = exchange(guess, "guess")

    weights, outer = call(
        functools.partial(weights_kernel, span, cap, deep),
        [f32_shape(span, hours, slots), f32_shape(span * deep, WIDE)],
        [WHOLE] * (3 + len(arrived)),
    )(here, beside, crossed, *arrived)
    piece = jnp.concatenate(
        [
            a[at : at + parts * cap]
            for k, ref in enumerate(arrived)
            for a, at in ((ref, 0), (crossed, chunk * k))
        ]
        + [outer],
        axis=0,
    )
    pieces = [piece] + [
        swap_by_core(piece, "tm", member_steps, k, "rows_members") for k in range(1, members)
    ]

    edge_rows = (3 * deep - 1) * span
    partial, diagonal, up, down = call(
        functools.partial(first_kernel, span, deep),
        [field_shape] * 2 + [f32_shape(blocks, edge_rows, LANES)] * 2,
        [SCALARS] * 2 + [WHOLE] * 9,
        flops=FIRST,
    )(
        index,
        ties,
        guess,
        right_side,
        diagonal_in,
        near_guess,
        far_guess,
        tile_high,
        tile_low,
        ramp_weight,
        bus_coupling,
    )
    before, after = adjacent_hours(up, down, "partial")

    sens_shape = jax.ShapeDtypeStruct((span, slots, width), BF16)
    deep_shape = f32_shape(blocks, rows + 2 * deep * span, LANES)
    next_shape = f32_shape(blocks, rows + 2 * (deep - 1) * span, LANES)
    residual, residual_sent, sens_high, sens_low, diagonal, owned_weight = call(
        functools.partial(owned_kernel, span, cap, deep),
        [
            deep_shape,
            next_shape,
            sens_shape,
            sens_shape,
            next_shape,
            f32_shape(span, hours + 2 * deep, slots),
        ],
        [SCALARS] + [WHOLE] * (9 + span),
        [pltpu.VMEM(deep_shape.shape, F32)] * 2,
    )(index, guess, partial, diagonal, weights, before, after, ramp_weight, here, beside, *pieces)

    def local_image(field, skip, earlier=None):
        shape = f32_shape(blocks, field.shape[1] - 2 * span, LANES)
        summed = earlier is not None
        return call(
            functools.partial(local_kernel, span, skip, summed),
            (shape, f32_shape(1, LANES)) if summed else shape,
            [SCALARS, SCALARS] + [WHOLE] * (9 + summed),
        )(
            index,
            ties,
            field,
            diagonal,
            ramp_weight,
            bus_coupling,
            tile_high,
            tile_low,
            sens_high,
            sens_low,
            owned_weight,
            *([earlier] if summed else []),
        )

    near, far = exchange(residual_sent, "residual")
    image = local_image(residual, 1)
    image, image_sent = call(
        functools.partial(cross_kernel, span, False),
        (f32_shape(*image.shape), field_shape),
        [SCALARS, SCALARS] + [WHOLE] * 6,
    )(index, ties, image, near, far, near_guess, far_guess, bus_coupling)

    near, far = exchange(image_sent, "image")
    second, sums = local_image(image, 2, residual)
    second, spread = call(
        functools.partial(cross_kernel, span, True),
        (field_shape, f32_shape(groups * members, LANES)),
        [SCALARS, SCALARS] + [WHOLE] * 8,
    )(index, ties, second, near, far, near_guess, far_guess, bus_coupling, image, sums)
    gathered = lax.all_to_all(spread, ("tm", "area"), split_axis=0, concat_axis=0, tiled=True)
    out_shape = f32_shape(hours, span, width)
    return tuple(
        call(
            last_kernel,
            (out_shape, out_shape),
            [WHOLE] * 5,
            [pltpu.VMEM((blocks, hours, span, LANES), F32)] * 2
            + [pltpu.SemaphoreType.DMA((2 * blocks,))],
            out_specs=[IN_HBM] * 2,
        )(gathered, guess, residual, image, second)
    )


def solution(mesh):
    field = P("tm", "area", None)
    placed = (
        field,
        P(),
        field,
        field,
        P("area", None, None),
        P("area", None),
        P("area", None),
        P(),
        P(),
        P("area", None),
        P("area", "tm"),
        P("area", None),
        field,
    )
    return jax.shard_map(
        body, mesh=mesh, in_specs=placed, out_specs=(field, field), check_vma=False
    )
```
